32 devices in a mesh: dp: 2 (over x), pipe: 4 (over z), expert: 4 (over y, core).
Axes of the slice: x: 2, y: 2, z: 4, core: 2. Of those that a mesh axis runs over, the one named last changes fastest.
Arguments:
- output_grads: bfloat16 [2, 4, 512, 4096], P('dp', 'pipe', 'expert'), may hold values from -4 to 4
- gate_values: float32 [2, 4, 512, 8], P('dp', 'pipe', 'expert'), may hold values from 0.1 to 1
- routing: int32 [2, 4, 512, 8], P('dp', 'pipe', 'expert'), may hold values from 0 to 127, as said below
- saved_inputs: bfloat16 [2, 4, 1, 4, 16, 4096], P('dp', 'pipe'), may hold values from -6 to 6
- expert_weights: bfloat16 [4, 3, 1536, 4096], P('pipe', None, 'expert'), may hold values from -0.09375 to 0.09375
Outputs:
- passed_grads: bfloat16 [2, 4, 512, 4096], P('dp', 'pipe', 'expert')
- weight_grads: bfloat16 [4, 3, 1536, 4096], P('pipe', None, 'expert', 'dp')
The draws below stay inside these ranges and needn't reach their ends.
Inputs may be any that keep to these rules, and one draw needn't show every extreme that they name: `routing`: each token names 8 different experts. Among the 128 tokens of one device (each aligned block of 128 tokens of a micro-batch), every expert below 1 is named by 1 to 16 tokens. In some replica and section, one such expert is named by exactly 16 tokens of every device of the expert axis.
All inputs are finite; a program needn't handle non-finite values.
Results may differ from the reference program's by a relative error of at most 0.014.
Values may be sent and summed in bfloat16 or wider, within the bound.
No kernel may reach another device: no remote copies, remote signals or barrier semaphores. Data moves between devices by JAX's collectives and lax.ppermute only.
A program may use at most 64 MiB of HBM per device.

```python
import functools
import jax
import jax.numpy as jnp
from jax import lax

D = 4096
EXPERTS = 128
TOP = 8
HIDDEN_SIZE = 1536
TOK = 128
CAP = 16
EXP_FLIGHT = 1
SPLIT = 4
HID_DEV = 384
WIN_ROWS = 1536
TOKENS = 512
N_DP = 2
N_PIPE = 4
N_EXPERT = 4


def draw_routing(key, part):
    groups = N_DP * N_PIPE
    blocks = groups * N_EXPERT
    subkeys = jax.random.split(key, 7)
    counts = jax.random.randint(subkeys[0], (blocks, EXP_FLIGHT), 1, CAP + 1)
    hottest = jnp.repeat(jax.random.randint(subkeys[1], (groups,), 0, EXP_FLIGHT), N_EXPERT)
    full_group = jax.random.randint(subkeys[5], (groups,), 0, 2)
    forced = jax.random.randint(subkeys[6], (), 0, groups)
    full_group = jnp.where(jnp.arange(groups) == forced, 1, full_group)
    full_block = jnp.repeat(full_group, N_EXPERT)
    expert_index = jnp.arange(EXP_FLIGHT)
    filled = (expert_index[None, :] == hottest[:, None]) & (full_block[:, None] == 1)
    counts = jnp.where(filled, CAP, counts)
    shuffle = jax.random.randint(subkeys[2], (blocks, EXP_FLIGHT, TOK), 0, 2 ** 20) * TOK + jnp.arange(TOK)
    ranking = jnp.argsort(jnp.argsort(shuffle, axis=-1), axis=-1)
    member = ranking < counts[:, :, None]
    window = jnp.transpose(member, (0, 2, 1))
    padded = jnp.concatenate([window, jnp.zeros((blocks, TOK, EXPERTS - EXP_FLIGHT), dtype=jnp.bool_)], axis=-1)
    columns = jnp.arange(EXPERTS)
    scores = jax.random.randint(subkeys[3], (blocks, TOK, EXPERTS), 0, 2 ** 20) * EXPERTS + columns
    scores = jnp.where(padded, 2 ** 30 + columns, jnp.where(columns < EXP_FLIGHT, -1, scores))
    top_scores, chosen = lax.top_k(scores, TOP)
    mixing = jax.random.randint(subkeys[4], (blocks, TOK, TOP), 0, 2 ** 20) * TOP + jnp.arange(TOP)
    column_order = jnp.argsort(mixing, axis=-1)
    chosen = jnp.take_along_axis(chosen, column_order, axis=-1)
    return chosen.reshape(N_DP, N_PIPE, N_EXPERT * TOK, TOP).astype(jnp.int32)


def shard_levels(rng, dims, pieces, low, largest):
    def one(axis_at, shards_of):
        draws = jax.random.uniform(jax.random.fold_in(jax.random.fold_in(rng, 6), axis_at), (shards_of,), jnp.float32, low / len(pieces), largest / len(pieces))
        return jnp.repeat(jnp.exp(draws), dims[axis_at] // shards_of).reshape((-1,) + (1,) * (len(dims) - axis_at - 1))

    level = one(*pieces[0])
    for cut in pieces[1:]:
        level = level * one(*cut)
    return level


def normal_values(stream_key, dims, spread, bound, cuts=(), kind=jnp.bfloat16):
    entries = spread * jax.random.normal(stream_key, dims, jnp.float32)
    if cuts:
        entries = entries * shard_levels(stream_key, dims, cuts, -0.22, 0.18)
    return jnp.clip(entries, -bound, bound).astype(kind)


def setup_inputs(seed: int = 0) -> dict:
    streams_of = jax.random.split(jax.random.key(seed), 6)
    output_grads = normal_values(streams_of[0], (N_DP, N_PIPE, TOKENS, D), 0.5, 4.0, ((0, 2), (1, 4), (2, 4)))
    gate_values = jnp.clip(0.1 + 0.9 * jax.random.uniform(streams_of[1], (N_DP, N_PIPE, TOKENS, TOP), jnp.float32) ** shard_levels(streams_of[1], (N_DP, N_PIPE, TOKENS, TOP), ((0, 2), (1, 4), (2, 4)), -0.2, 0.2), 0.1, 1.0)
    routing = draw_routing(jax.random.fold_in(streams_of[5], 71), 0)
    saved_inputs = normal_values(streams_of[3], (N_DP, N_PIPE, EXP_FLIGHT, N_EXPERT, CAP, D), 1.0, 6.0, ((0, 2), (1, 4)))
    expert_weights = normal_values(streams_of[4], (N_PIPE, 3, WIN_ROWS, D), D ** -0.5, 0.09375, ((0, 4), (2, 4)))
    return dict(output_grads=output_grads, gate_values=gate_values, routing=routing, saved_inputs=saved_inputs, expert_weights=expert_weights)


def route_tables(routing, gate_values, flight, capacity):
    expert_index = jnp.arange(flight, dtype=jnp.int32)
    matches = routing[:, :, None] == expert_index[None, None, :]
    member = jnp.any(matches, axis=1)
    gate_share = jnp.sum(jnp.where(matches, gate_values[:, :, None], jnp.float32(0.0)), axis=1)
    member_count = member.astype(jnp.int32)
    slot_index = jnp.cumsum(member_count, axis=0) - member_count
    chooser = (slot_index[None, :, :] == jnp.arange(capacity, dtype=jnp.int32)[:, None, None]) & member[None, :, :]
    selector = jnp.transpose(chooser, (2, 0, 1))
    return member, slot_index, gate_share, selector


def group_pass(section_grads, section_routing, section_gates, section_saved, weights_section):
    sources = section_grads.reshape(N_EXPERT, TOK, D)
    tables = jax.vmap(functools.partial(route_tables, flight=EXP_FLIGHT, capacity=CAP))
    member, slot_index, gate_share, selector = tables(section_routing.reshape(N_EXPERT, TOK, TOP), section_gates.reshape(N_EXPERT, TOK, TOP))
    picked = jnp.einsum('sect,std->secd', selector.astype(jnp.float32), sources.astype(jnp.float32), precision=lax.Precision.HIGHEST)
    weighting = jnp.sum(jnp.where(selector, jnp.transpose(gate_share, (0, 2, 1))[:, :, None, :], jnp.float32(0.0)), axis=-1)
    routed = (picked * weighting[:, :, :, None]).astype(jnp.bfloat16)
    summed_list = []
    grad_list = []
    by_rows = (((0,), (0,)), ((), ()))
    for expert in range(EXP_FLIGHT):
        own_inputs = section_saved[expert].reshape(N_EXPERT * CAP, D)
        routed_rows = routed[:, expert].reshape(N_EXPERT * CAP, D)
        base = expert * HIDDEN_SIZE
        gate_weight = weights_section[0, base:base + HIDDEN_SIZE]
        up_weight = weights_section[1, base:base + HIDDEN_SIZE]
        down_weight = weights_section[2, base:base + HIDDEN_SIZE]
        gate_pre = jnp.dot(own_inputs, gate_weight.T, preferred_element_type=jnp.float32)
        up_pre = jnp.dot(own_inputs, up_weight.T, preferred_element_type=jnp.float32)
        sigmoid_gate = jax.nn.sigmoid(gate_pre)
        activated = gate_pre * sigmoid_gate
        hidden = (activated * up_pre).astype(jnp.bfloat16)
        hidden_grad = jnp.dot(routed_rows, down_weight.T, preferred_element_type=jnp.float32)
        gate_grad = (hidden_grad * up_pre * sigmoid_gate * (1.0 + gate_pre * (1.0 - sigmoid_gate))).astype(jnp.bfloat16)
        up_grad = (hidden_grad * activated).astype(jnp.bfloat16)
        rows_count = N_EXPERT * CAP
        partial_gate = jnp.einsum('rsh,shd->rsd', gate_grad.reshape(rows_count, SPLIT, HID_DEV).astype(jnp.float32), gate_weight.reshape(SPLIT, HID_DEV, D).astype(jnp.float32), precision=lax.Precision.HIGHEST)
        partial_up = jnp.einsum('rsh,shd->rsd', up_grad.reshape(rows_count, SPLIT, HID_DEV).astype(jnp.float32), up_weight.reshape(SPLIT, HID_DEV, D).astype(jnp.float32), precision=lax.Precision.HIGHEST)
        partial_value = lax.optimization_barrier((partial_gate + partial_up).astype(jnp.bfloat16))
        summed = jnp.sum(partial_value.astype(jnp.float32), axis=1)
        summed_list.append(summed.reshape(N_EXPERT, CAP, D))
        grad_gate = lax.dot_general(gate_grad, own_inputs, by_rows, preferred_element_type=jnp.float32)
        grad_up = lax.dot_general(up_grad, own_inputs, by_rows, preferred_element_type=jnp.float32)
        grad_down = lax.dot_general(hidden, routed_rows, by_rows, preferred_element_type=jnp.float32)
        grad_list.append(jnp.stack([grad_gate, grad_up, grad_down]))
    summed_all = jnp.stack(summed_list, axis=1)
    source_index = jnp.arange(N_EXPERT, dtype=jnp.int32)[:, None, None]
    expert_index = jnp.arange(EXP_FLIGHT, dtype=jnp.int32)[None, None, :]
    clipped = jnp.minimum(slot_index, CAP - 1)
    gathered = summed_all[source_index, expert_index, clipped]
    added = jnp.sum(jnp.where(member[:, :, :, None], gathered, jnp.float32(0.0)), axis=2)
    input_grads = (sources.astype(jnp.float32) + added).astype(jnp.bfloat16).reshape(TOKENS, D)
    replica_grads = jnp.concatenate(grad_list, axis=1).astype(jnp.bfloat16)
    return input_grads, replica_grads


def reference(output_grads, gate_values, routing, saved_inputs, expert_weights):
    def per_section(section):
        weights_section = lax.dynamic_index_in_dim(expert_weights, section, 0, keepdims=False)
        total = jnp.zeros((3, WIN_ROWS, D), jnp.float32)
        results = []
        for replica in range(N_DP):
            section_grads = lax.dynamic_index_in_dim(output_grads[replica], section, 0, keepdims=False)
            section_gates = lax.dynamic_index_in_dim(gate_values[replica], section, 0, keepdims=False)
            section_routing = lax.dynamic_index_in_dim(routing[replica], section, 0, keepdims=False)
            section_saved = lax.dynamic_index_in_dim(saved_inputs[replica], section, 0, keepdims=False)
            input_grads, replica_grads = group_pass(section_grads, section_routing, section_gates, section_saved, weights_section)
            total = total + replica_grads.astype(jnp.float32)
            results.append(input_grads)
        return jnp.stack(results), total.astype(jnp.bfloat16)

    all_inputs, weight_grads = lax.map(per_section, jnp.arange(N_PIPE, dtype=jnp.int32))
    all_inputs = jnp.transpose(all_inputs, (1, 0, 2, 3))
    passed_grads = jnp.roll(all_inputs, -1, axis=1)
    return passed_grads, weight_grads
```

```python
import jax
import jax.numpy as jnp
from jax import lax
from jax.sharding import PartitionSpec as P


def partner(index, step, count):
    if count & (count - 1) == 0:
        return index ^ step
    return (index + step) % count


def origin(index, step, count):
    if count & (count - 1) == 0:
        return index ^ step
    return (index - step) % count


def exchange(value, axis, step):
    count = lax.axis_size(axis)
    return lax.ppermute(value, axis, [(i, partner(i, step, count)) for i in range(count)])


def to_previous(value):
    count = lax.axis_size("pipe")
    return lax.ppermute(value, "pipe", [(i, (i - 1) % count) for i in range(count)])


def route_tables(routing, gate_values, capacity):
    matches = routing == 0
    member = jnp.any(matches, axis=1)
    count = member.astype(jnp.int32)
    slot = jnp.cumsum(count) - count
    share = jnp.sum(jnp.where(matches, gate_values, jnp.float32(0.0)), axis=1)
    selector = (slot[None, :] == jnp.arange(capacity, dtype=jnp.int32)[:, None]) & member[None, :]
    return member, slot, share, selector


def shards(output_grads, gate_values, routing, saved_inputs, expert_weights):
    owners = lax.axis_size("expert")
    replicas = lax.axis_size("dp")
    capacity = saved_inputs.shape[4]
    incoming = output_grads[0, 0]
    width = incoming.shape[1]
    part = width // replicas
    me = lax.axis_index("expert")
    replica = lax.axis_index("dp")

    shifted = to_previous(incoming)
    next_routing = to_previous(routing[0, 0])

    saved = saved_inputs[0, 0, 0]
    own_inputs = jnp.concatenate(
        [lax.dynamic_index_in_dim(saved, origin(me, k, owners), 0, keepdims=False) for k in range(owners)]
    )

    def columns_of(rows, who):
        return lax.dynamic_slice_in_dim(rows, who * part, part, axis=1)

    def across(rows):
        return [
            exchange(columns_of(rows, partner(replica, k, replicas)), "dp", k) for k in range(1, replicas)
        ]

    far_inputs = across(own_inputs)

    member, slot, share, selector = route_tables(routing[0, 0], gate_values[0, 0], capacity)
    picked = jnp.dot(selector.astype(jnp.bfloat16), incoming, preferred_element_type=jnp.float32)
    weighting = jnp.sum(jnp.where(selector, share[None, :], jnp.float32(0.0)), axis=-1)
    routed = (picked * weighting[:, None]).astype(jnp.bfloat16)
    arrived = [routed] + [exchange(routed, "expert", k) for k in range(1, owners)]

    gate_weight, up_weight, down_weight = expert_weights[0, 0], expert_weights[0, 1], expert_weights[0, 2]
    contract = (((1,), (1,)), ((), ()))
    gate_pre = lax.dot_general(own_inputs, gate_weight, contract, preferred_element_type=jnp.float32)
    up_pre = lax.dot_general(own_inputs, up_weight, contract, preferred_element_type=jnp.float32)
    sigmoid_gate = jax.nn.sigmoid(gate_pre)
    activated = gate_pre * sigmoid_gate
    hidden = (activated * up_pre).astype(jnp.bfloat16)
    slope = up_pre * sigmoid_gate * (1.0 + gate_pre * (1.0 - sigmoid_gate))

    routed_rows = jnp.concatenate(arrived)
    hidden_grad = lax.dot_general(
        routed_rows, down_weight, contract, preferred_element_type=jnp.float32
    )
    gate_grad = (hidden_grad * slope).astype(jnp.bfloat16)
    up_grad = (hidden_grad * activated).astype(jnp.bfloat16)
    partial_value = (
        jnp.dot(gate_grad, gate_weight, preferred_element_type=jnp.float32)
        + jnp.dot(up_grad, up_weight, preferred_element_type=jnp.float32)
    ).astype(jnp.bfloat16)
    blocks = partial_value.reshape(owners, capacity, width)
    summed = blocks[0].astype(jnp.float32)
    for k in range(1, owners):
        summed = summed + exchange(blocks[k], "expert", k).astype(jnp.float32)
    changed = (picked + summed).astype(jnp.bfloat16)
    next_changed = to_previous(changed)

    far_rows = across(routed_rows)
    factors = jnp.concatenate([gate_grad, up_grad, hidden], axis=1)
    far_factors = [exchange(factors, "dp", k) for k in range(1, replicas)]
    inputs_all = jnp.concatenate([columns_of(own_inputs, replica)] + far_inputs)
    rows_all = jnp.concatenate([columns_of(routed_rows, replica)] + far_rows)
    factors_all = jnp.concatenate([factors] + far_factors)
    hid = gate_weight.shape[0]
    by_rows = (((0,), (0,)), ((), ()))
    weight_grads = jnp.stack(
        [
            lax.dot_general(
                factors_all[:, i * hid : (i + 1) * hid],
                rows_all if i == 2 else inputs_all,
                by_rows,
                preferred_element_type=jnp.float32,
            ).astype(jnp.bfloat16)
            for i in range(3)
        ]
    )[None]

    next_member, next_slot, _, next_selector = route_tables(
        next_routing, jnp.zeros(next_routing.shape, jnp.float32), capacity
    )
    placed = jnp.dot(
        jnp.transpose(next_selector).astype(jnp.bfloat16), next_changed, preferred_element_type=jnp.float32
    ).astype(jnp.bfloat16)
    passed_grads = jnp.where(next_member[:, None], placed, shifted)[None, None]
    return (passed_grads, weight_grads)


def solution(mesh):
    placed = (
        P("dp", "pipe", "expert", None),
        P("dp", "pipe", "expert", None),
        P("dp", "pipe", "expert", None),
        P("dp", "pipe", None, None, None, None),
        P("pipe", None, "expert", None),
    )
    return jax.shard_map(
        shards,
        mesh=mesh,
        in_specs=placed,
        out_specs=(P("dp", "pipe", "expert", None), P("pipe", None, "expert", "dp")),
        check_vma=False,
    )
```

```python
import functools

import jax
import jax.numpy as jnp
from jax import lax
from jax.experimental import pallas as pl
from jax.experimental.pallas import tpu as pltpu
from jax.sharding import PartitionSpec as P

BF16 = jnp.bfloat16
F32 = jnp.float32
LANES = 128
VMEM_LIMIT = 20 * 2**20
LAST_LAST = (((1,), (1,)), ((), ()))
FIRST_FIRST = (((0,), (0,)), ((), ()))
ROWS_COLS = (((1,), (0,)), ((), ()))


def partner(index, step, count):
    if count & (count - 1) == 0:
        return index ^ step
    return (index + step) % count


def origin(index, step, count):
    if count & (count - 1) == 0:
        return index ^ step
    return (index - step) % count


def exchange(value, axis, step):
    count = lax.axis_size(axis)
    return lax.ppermute(value, axis, [(i, partner(i, step, count)) for i in range(count)])


def to_previous(value):
    count = lax.axis_size("pipe")
    return lax.ppermute(value, "pipe", [(i, (i - 1) % count) for i in range(count)])


def mm(left, right, dims):
    return lax.dot_general(left, right, dims, preferred_element_type=F32)


def run(body, name, outs, inputs, flops, scalars=0, grid=None, in_specs=None, out_specs=None):
    vmem = pl.BlockSpec(memory_space=pltpu.VMEM)
    smem = pl.BlockSpec(memory_space=pltpu.SMEM)
    moved = sum(v.size * v.dtype.itemsize for v in (*inputs, *outs))
    extra = {} if grid is None else {"grid": grid}
    return pl.pallas_call(
        body,
        name=name,
        out_shape=outs,
        in_specs=in_specs or [smem] * scalars + [vmem] * (len(inputs) - scalars),
        out_specs=out_specs or [vmem] * len(outs),
        compiler_params=pltpu.CompilerParams(vmem_limit_bytes=VMEM_LIMIT),
        cost_estimate=pl.CostEstimate(flops=flops, bytes_accessed=moved, transcendentals=0),
        **extra,
    )(*inputs)


def route_body(routing_ref, gates_ref, incoming_ref, routed_ref, picked_ref, ids_ref):
    capacity = routed_ref.shape[0]
    tokens = incoming_ref.shape[0]
    matches = routing_ref[...] == 0
    member = jnp.max(jnp.where(matches, F32(1.0), F32(0.0)), axis=0, keepdims=True)
    share = jnp.sum(jnp.where(matches, gates_ref[...], F32(0.0)), axis=0, keepdims=True)
    earlier = lax.broadcasted_iota(jnp.int32, (tokens, tokens), 0) < lax.broadcasted_iota(
        jnp.int32, (tokens, tokens), 1
    )
    spread = jnp.broadcast_to(member, (capacity, tokens))
    slot = mm(spread.astype(BF16), jnp.where(earlier, F32(1.0), F32(0.0)).astype(BF16), ROWS_COLS)
    wanted = lax.broadcasted_iota(jnp.int32, (capacity, tokens), 0).astype(F32)
    chosen = jnp.where((slot == wanted) & (spread > 0.5), F32(1.0), F32(0.0))
    weighting = jnp.sum(chosen * share, axis=1, keepdims=True)
    picked = mm(chosen.astype(BF16), incoming_ref[...], ROWS_COLS)
    routed_ref[...] = (picked * weighting).astype(BF16)
    picked_ref[...] = picked.astype(BF16)
    token = lax.broadcasted_iota(jnp.int32, (capacity, tokens), 1)
    filled = jnp.sum(chosen, axis=1, keepdims=True)
    high = jnp.sum(chosen * (token // LANES).astype(F32), axis=1, keepdims=True)
    low = jnp.sum(chosen * (token % LANES).astype(F32), axis=1, keepdims=True)
    high = jnp.where(filled > 0.5, high, F32(-1.0))
    lane = lax.broadcasted_iota(jnp.int32, (capacity, LANES), 1)
    ids_ref[...] = jnp.where(lane == 0, high, jnp.where(lane == 1, low, F32(0.0))).astype(BF16)


def forward_body(order, others, who_ref, inputs_ref, weights_ref, *outs):
    slope_ref, active_ref, hidden_ref, own_ref = outs[:4]
    part = own_ref.shape[1]
    rows = jnp.concatenate([inputs_ref[who_ref[k]] for k in range(order)], axis=0)
    gate_pre = mm(weights_ref[0], rows, LAST_LAST)
    up_pre = mm(weights_ref[1], rows, LAST_LAST)
    sigmoid_gate = jax.nn.sigmoid(gate_pre)
    activated = gate_pre * sigmoid_gate
    slope_ref[...] = up_pre * sigmoid_gate * (1.0 + gate_pre * (1.0 - sigmoid_gate))
    active_ref[...] = activated
    hidden = jnp.transpose(activated * up_pre).astype(BF16)
    hidden_ref[...] = hidden
    capacity = inputs_ref.shape[1]
    for r in range(others + 1):
        first = pl.multiple_of(who_ref[order + r], LANES)
        into = own_ref if r == 0 else outs[3 + r]
        for k in range(order):
            into[k * capacity : (k + 1) * capacity, :part] = inputs_ref[who_ref[k], :, pl.ds(first, part)]
        if r:
            into[:, part:] = hidden


def backward_body(order, others, who_ref, *refs):
    blocks = refs[:order]
    weights_ref, slope_ref, active_ref = refs[order : order + 3]
    outs = refs[order + 3 :]
    partials, grads_ref, own_ref, fars = outs[:order], outs[order], outs[order + 1], outs[order + 2 :]
    part = own_ref.shape[1]
    rows = jnp.concatenate([b[...] for b in blocks], axis=0)
    hidden_grad = mm(weights_ref[2], rows, LAST_LAST)
    gate_grad = jnp.transpose(hidden_grad * slope_ref[...]).astype(BF16)
    up_grad = jnp.transpose(hidden_grad * active_ref[...]).astype(BF16)
    grads = jnp.concatenate([gate_grad, up_grad], axis=1)
    grads_ref[...] = grads
    hid = weights_ref.shape[1]
    capacity = blocks[0].shape[0]
    width = blocks[0].shape[1]
    step = 512
    for c in range(width // step):
        at = slice(c * step, (c + 1) * step)
        total = mm(gate_grad, weights_ref[0, :, at], ROWS_COLS) + mm(up_grad, weights_ref[1, :, at], ROWS_COLS)
        for k in range(order):
            partials[k][:, at] = total[k * capacity : (k + 1) * capacity].astype(BF16)
    for r in range(others + 1):
        first = pl.multiple_of(who_ref[r], LANES)
        into = own_ref if r == 0 else fars[r - 1]
        for k in range(order):
            into[k * capacity : (k + 1) * capacity, :part] = blocks[k][:, pl.ds(first, part)]
        if r:
            into[:, part:] = grads


def return_body(order, *refs):
    picked_ref, ids_ref, out_ref = refs[0], refs[1], refs[-1]
    width = picked_ref.shape[1]
    total = picked_ref[...].astype(F32)
    back = refs[2][...].astype(F32)
    for ref in refs[3 : 2 + order]:
        back = back + ref[...].astype(F32)
    out_ref[:, :width] = (total + back).astype(BF16)
    out_ref[:, width:] = ids_ref[...]


def weight_body(others, hidden_ref, grads_ref, inputs_ref, rows_ref, *refs):
    fars_in, fars_out, out_ref = refs[:others], refs[others : 2 * others], refs[2 * others]
    part = inputs_ref.shape[1]
    hid = hidden_ref.shape[1]
    kind = pl.program_id(0)

    def product(lefts, rights):
        left = jnp.concatenate(lefts, axis=0)
        right = jnp.concatenate(rights, axis=0)
        out_ref[0, 0] = mm(left, right, FIRST_FIRST).astype(BF16)

    for i in range(2):

        @pl.when(kind == i)
        def _(i=i):
            product(
                [grads_ref[:, i * hid : (i + 1) * hid]]
                + [f[:, part + i * hid : part + (i + 1) * hid] for f in fars_out],
                [inputs_ref[...]] + [f[:, :part] for f in fars_in],
            )

    @pl.when(kind == 2)
    def _():
        product(
            [hidden_ref[...]] + [f[:, part:] for f in fars_in],
            [rows_ref[...]] + [f[:, :part] for f in fars_out],
        )


def merge_body(shifted_ref, changed_ref, out_ref):
    tokens, width = shifted_ref.shape
    capacity = changed_ref.shape[0]
    high = changed_ref[:, width : width + 1].astype(F32)
    low = changed_ref[:, width + 1 : width + 2].astype(F32)
    token = lax.broadcasted_iota(jnp.int32, (capacity, tokens), 1).astype(F32)
    chosen = jnp.where(token == high * F32(LANES) + low, F32(1.0), F32(0.0)).astype(BF16)
    here = mm(chosen, jnp.ones((capacity, LANES), BF16), FIRST_FIRST)[:, :1] > 0.5
    step = 1024
    for c in range(width // step):
        at = slice(c * step, (c + 1) * step)
        placed = mm(chosen, changed_ref[:, at], FIRST_FIRST)
        out_ref[0, 0, :, at] = jnp.where(here, placed, shifted_ref[:, at].astype(F32)).astype(BF16)


def shards(output_grads, gate_values, routing, saved_inputs, expert_weights):
    owners = lax.axis_size("expert")
    replicas = lax.axis_size("dp")
    others = replicas - 1
    capacity = saved_inputs.shape[4]
    incoming = output_grads[0, 0]
    tokens, width = incoming.shape
    part = width // replicas
    weights = expert_weights[0]
    hid = weights.shape[1]
    rows = owners * capacity
    me = lax.axis_index("expert")
    replica = lax.axis_index("dp")
    out = jax.ShapeDtypeStruct

    shifted = to_previous(incoming)

    routed, picked, ids = run(
        route_body,
        "route",
        [out((capacity, width), BF16), out((capacity, width), BF16), out((capacity, LANES), BF16)],
        [jnp.transpose(routing[0, 0]), jnp.transpose(gate_values[0, 0]), incoming],
        2 * capacity * tokens * width,
    )
    arrived = [exchange(routed, "expert", k) for k in reversed(range(1, owners))][::-1]

    sources = jnp.stack([origin(me, k, owners) for k in range(owners)]).astype(jnp.int32)
    columns = jnp.stack([partner(replica, k, replicas) * part for k in range(replicas)]).astype(jnp.int32)
    far_in = out((rows, part + hid), BF16)
    slope, active, hidden, own_inputs, *fars = run(
        functools.partial(forward_body, owners, others),
        "forward",
        [out((hid, rows), F32), out((hid, rows), F32), out((rows, hid), BF16), out((rows, part), BF16)]
        + [far_in] * others,
        [jnp.concatenate([sources, columns]), saved_inputs[0, 0, 0], weights],
        4 * rows * hid * width,
        scalars=1,
    )
    far_inputs = [exchange(f, "dp", k + 1) for k, f in enumerate(fars)]

    results = run(
        functools.partial(backward_body, owners, others),
        "backward",
        [out((capacity, width), BF16)] * owners
        + [out((rows, 2 * hid), BF16), out((rows, part), BF16)]
        + [out((rows, part + 2 * hid), BF16)] * others,
        [columns, routed, *arrived, weights, slope, active],
        6 * rows * hid * width,
        scalars=1,
    )
    partials, grads, own_rows, fars = (
        results[:owners],
        results[owners],
        results[owners + 1],
        results[owners + 2 :],
    )
    returned = [exchange(partials[k], "expert", k) for k in reversed(range(1, owners))][::-1]
    far_rows = [exchange(f, "dp", k + 1) for k, f in enumerate(fars)]

    changed = run(
        functools.partial(return_body, owners),
        "sum_returned",
        [out((capacity, width + LANES), BF16)],
        [picked, ids, partials[0], *returned],
        0,
    )[0]
    next_changed = to_previous(changed)

    whole = lambda v: pl.BlockSpec(v.shape, lambda i: (0,) * len(v.shape))
    operands = [hidden, grads, own_inputs, own_rows, *far_inputs, *far_rows]
    weight_grads = run(
        functools.partial(weight_body, others),
        "weight_grads",
        [out((1, 3, hid, part), BF16)],
        operands,
        6 * rows * replicas * hid * part,
        grid=(3,),
        in_specs=[whole(v) for v in operands],
        out_specs=[pl.BlockSpec((1, 1, hid, part), lambda i: (0, i, 0, 0))],
    )[0]

    passed_grads = run(
        merge_body,
        "merge",
        [out((1, 1, tokens, width), BF16)],
        [shifted, next_changed],
        2 * capacity * tokens * width,
    )[0]
    return (passed_grads, weight_grads)


def solution(mesh):
    placed = (
        P("dp", "pipe", "expert", None),
        P("dp", "pipe", "expert", None),
        P("dp", "pipe", "expert", None),
        P("dp", "pipe", None, None, None, None),
        P("pipe", None, "expert", None),
    )
    return jax.shard_map(
        shards,
        mesh=mesh,
        in_specs=placed,
        out_specs=(P("dp", "pipe", "expert", None), P("pipe", None, "expert", "dp")),
        check_vma=False,
    )
```

```python
import functools

import jax
import jax.numpy as jnp
from jax import lax
from jax.experimental import pallas as pl
from jax.experimental.pallas import tpu as pltpu
from jax.sharding import PartitionSpec as P

BF16 = jnp.bfloat16
F32 = jnp.float32
LANES = 128
VMEM_LIMIT = 20 * 2**20
SUM_COST = 0
ROUTE_COST = 10**10
LAST_LAST = (((1,), (1,)), ((), ()))
FIRST_FIRST = (((0,), (0,)), ((), ()))
ROWS_COLS = (((1,), (0,)), ((), ()))


def partner(index, step, count):
    if count & (count - 1) == 0:
        return index ^ step
    return (index + step) % count


def origin(index, step, count):
    if count & (count - 1) == 0:
        return index ^ step
    return (index - step) % count


def pairs_of(owners):
    inner = 2 if owners % 2 == 0 else 1
    return inner, owners // inner


def source(me, block, owners):
    inner, outer = pairs_of(owners)
    return origin(me // inner, block // inner, outer) * inner + (me % inner ^ block % inner)


def exchange(value, axis, step):
    count = lax.axis_size(axis)
    return lax.ppermute(value, axis, [(i, partner(i, step, count)) for i in range(count)])


def to_sibling(value):
    return lax.ppermute(value, "expert", [(i, i ^ 1) for i in range(lax.axis_size("expert"))])


def to_pair(value, step, back=False):
    owners = lax.axis_size("expert")
    inner, outer = pairs_of(owners)
    hops = [(i, partner(i // inner, step, outer) * inner + i % inner) for i in range(owners)]
    return lax.ppermute(value, "expert", [(j, i) for i, j in hops] if back else hops)


def to_previous(value):
    count = lax.axis_size("pipe")
    return lax.ppermute(value, "pipe", [(i, (i - 1) % count) for i in range(count)])


def mm(left, right, dims):
    return lax.dot_general(left, right, dims, preferred_element_type=F32)


def run(body, name, outs, inputs, flops, in_specs=None, out_specs=None, scratch=()):
    vmem = pl.BlockSpec(memory_space=pltpu.VMEM)
    moved = sum(v.size * v.dtype.itemsize for v in inputs)
    return pl.pallas_call(
        body,
        name=name,
        out_shape=outs,
        in_specs=in_specs or [vmem] * len(inputs),
        out_specs=out_specs or [vmem] * len(outs),
        scratch_shapes=scratch,
        compiler_params=pltpu.CompilerParams(vmem_limit_bytes=VMEM_LIMIT),
        cost_estimate=pl.CostEstimate(flops=flops, bytes_accessed=moved, transcendentals=0),
    )(*inputs)


def in_hbm(value):
    return pltpu.with_memory_space_constraint(value, pltpu.HBM)


def route_body(routing_hbm, gates_hbm, incoming_hbm, saved_hbm, *refs):
    others = lax.axis_size("dp") - 1
    owners = lax.axis_size("expert")
    routed_ref, picked_ref, ids_ref = refs[:3]
    fars = refs[3 : 3 + others]
    routing_ref, gates_ref, incoming_ref, sems, far_sem = refs[3 + others :]
    capacity = routed_ref.shape[0]
    tokens, width = incoming_ref.shape
    me = lax.axis_index("expert")
    replica = lax.axis_index("dp")
    fetches = [
        pltpu.make_async_copy(routing_hbm, routing_ref, sems.at[0]),
        pltpu.make_async_copy(gates_hbm, gates_ref, sems.at[1]),
        pltpu.make_async_copy(incoming_hbm, incoming_ref, sems.at[2]),
    ]
    for f in fetches:
        f.start()
    copies = []
    for r in range(others):
        part = fars[r].shape[1]
        first = pl.multiple_of(partner(replica, r + 1, others + 1) * part, LANES)
        for k in range(owners):
            copies.append(
                pltpu.make_async_copy(
                    saved_hbm.at[source(me, k, owners), :, pl.ds(first, part)],
                    fars[r].at[pl.ds(k * capacity, capacity)],
                    far_sem.at[r, k],
                )
            )
    for c in copies:
        c.start()
    fetches[0].wait()
    fetches[1].wait()
    matches = routing_ref[...] == 0
    member = jnp.max(jnp.where(matches, F32(1.0), F32(0.0)), axis=0, keepdims=True)
    share = jnp.sum(jnp.where(matches, gates_ref[...], F32(0.0)), axis=0, keepdims=True)
    earlier = lax.broadcasted_iota(jnp.int32, (tokens, tokens), 0) < lax.broadcasted_iota(
        jnp.int32, (tokens, tokens), 1
    )
    spread = jnp.broadcast_to(member, (capacity, tokens))
    slot = mm(spread.astype(BF16), jnp.where(earlier, F32(1.0), F32(0.0)).astype(BF16), ROWS_COLS)
    wanted = lax.broadcasted_iota(jnp.int32, (capacity, tokens), 0).astype(F32)
    chosen = jnp.where((slot == wanted) & (spread > 0.5), F32(1.0), F32(0.0))
    weighting = jnp.sum(chosen * share, axis=1, keepdims=True)
    token = lax.broadcasted_iota(jnp.int32, (capacity, tokens), 1)
    filled = jnp.sum(chosen, axis=1, keepdims=True)
    high = jnp.sum(chosen * (token // LANES).astype(F32), axis=1, keepdims=True)
    low = jnp.sum(chosen * (token % LANES).astype(F32), axis=1, keepdims=True)
    high = jnp.where(filled > 0.5, high, F32(-1.0))
    lane = lax.broadcasted_iota(jnp.int32, (capacity, LANES), 1)
    ids_ref[...] = jnp.where(lane == 0, high, jnp.where(lane == 1, low, F32(0.0))).astype(BF16)
    fetches[2].wait()
    picked = mm(chosen.astype(BF16), incoming_ref[...], ROWS_COLS)
    routed_ref[...] = (picked * weighting).astype(BF16)
    picked_ref[...] = picked.astype(BF16)
    for c in copies:
        c.wait()


def forward_body(saved_hbm, weights_ref, slope_ref, active_ref, hidden_ref, own_ref, rows_ref, row_sem):
    owners, capacity, width = saved_hbm.shape
    part = own_ref.shape[1]
    me = lax.axis_index("expert")
    replica = lax.axis_index("dp")
    fetches = []
    for k in range(owners):
        fetches.append(
            pltpu.make_async_copy(
                saved_hbm.at[source(me, k, owners)],
                rows_ref.at[pl.ds(k * capacity, capacity)],
                row_sem.at[k],
            )
        )
    for f in fetches:
        f.start()
    for f in fetches:
        f.wait()
    rows = rows_ref[...]
    gate_pre = mm(weights_ref[0], rows, LAST_LAST)
    up_pre = mm(weights_ref[1], rows, LAST_LAST)
    sigmoid_gate = jax.nn.sigmoid(gate_pre)
    activated = gate_pre * sigmoid_gate
    slope_ref[...] = up_pre * sigmoid_gate * (1.0 + gate_pre * (1.0 - sigmoid_gate))
    active_ref[...] = activated
    hidden_ref[...] = jnp.transpose(activated * up_pre).astype(BF16)
    own_ref[...] = rows_ref[:, pl.ds(pl.multiple_of(replica * part, LANES), part)]


def backward_body(order, *refs):
    blocks = refs[:order]
    weights_ref, slope_ref, active_ref = refs[order : order + 3]
    kept_ref, given_ref, grads_ref = refs[-3:]
    inner, outer = pairs_of(order)
    rows = jnp.concatenate([b[...] for b in blocks], axis=0)
    hidden_grad = mm(weights_ref[2], rows, LAST_LAST)
    gate_grad = jnp.transpose(hidden_grad * slope_ref[...]).astype(BF16)
    up_grad = jnp.transpose(hidden_grad * active_ref[...]).astype(BF16)
    capacity, width = blocks[0].shape
    step = 512
    for c in range(width // step):
        at = slice(c * step, (c + 1) * step)
        total = mm(gate_grad, weights_ref[0, :, at], ROWS_COLS) + mm(up_grad, weights_ref[1, :, at], ROWS_COLS)
        for k in range(order):
            into = kept_ref if k % inner == 0 else given_ref
            j = k // inner
            into[j * capacity : (j + 1) * capacity, at] = total[k * capacity : (k + 1) * capacity].astype(BF16)
    hid = weights_ref.shape[1]
    grads_ref[:, :hid] = gate_grad
    grads_ref[:, hid:] = up_grad


def pair_body(paired, kept_ref, given_ref, *outs):
    capacity = outs[0].shape[0]
    for j, ref in enumerate(outs, 1):
        at = slice(j * capacity, (j + 1) * capacity)
        total = kept_ref[at].astype(F32)
        ref[...] = (total + given_ref[at].astype(F32) if paired else total).astype(BF16)


def pack_body(order, *refs):
    blocks = refs[:order]
    hidden_ref, grads_ref, _ = refs[order : order + 3]
    own_ref, fars = refs[order + 3], refs[order + 4 :]
    capacity = blocks[0].shape[0]
    part = own_ref.shape[1]
    replica = lax.axis_index("dp")
    for r in range(len(fars) + 1):
        first = pl.multiple_of(partner(replica, r, len(fars) + 1) * part, LANES)
        into = own_ref if r == 0 else fars[r - 1]
        for k in range(order):
            into[k * capacity : (k + 1) * capacity, :part] = blocks[k][:, pl.ds(first, part)]
        if r:
            hid = hidden_ref.shape[1]
            into[:, part : part + 2 * hid] = grads_ref[...]
            into[:, part + 2 * hid :] = hidden_ref[...]


def return_body(paired, picked_ref, ids_ref, kept_ref, given_ref, *refs):
    returned, out_ref = refs[:-1], refs[-1]
    capacity, width = picked_ref.shape
    back = kept_ref[:capacity].astype(F32)
    if paired:
        back = back + given_ref[:capacity].astype(F32)
    for ref in returned:
        back = back + ref[...].astype(F32)
    out_ref[:, :width] = (picked_ref[...].astype(F32) + back).astype(BF16)
    out_ref[:, width:] = ids_ref[...]


def weight_body(others, hidden_ref, grads_ref, inputs_ref, rows_ref, *refs):
    fars_in, fars_out = refs[:others], refs[others : 2 * others]
    out_hbm, held, sems = refs[2 * others :]
    part = inputs_ref.shape[1]
    hid = hidden_ref.shape[1]
    columns = held.shape[2]
    left = [
        jnp.concatenate(
            [grads_ref[:, i * hid : (i + 1) * hid] if i < 2 else hidden_ref[...]]
            + [f[:, part + i * hid : part + (i + 1) * hid] for f in fars_out],
            axis=0,
        )
        for i in range(3)
    ]
    copies = []
    for c in range(part // columns):
        at = slice(c * columns, (c + 1) * columns)
        inputs = jnp.concatenate([inputs_ref[:, at]] + [f[:, at] for f in fars_in], axis=0)
        rows = jnp.concatenate([rows_ref[:, at]] + [f[:, at] for f in fars_out], axis=0)
        for i in range(3):
            n = len(copies)
            held[n] = mm(left[i], rows if i == 2 else inputs, FIRST_FIRST).astype(BF16)
            copies.append(pltpu.make_async_copy(held.at[n], out_hbm.at[0, i, :, pl.ds(c * columns, columns)], sems.at[n]))
            copies[-1].start()
    for c in copies:
        c.wait()


def merge_body(shifted_ref, changed_ref, out_hbm, held, sems):
    tokens, width = shifted_ref.shape
    capacity = changed_ref.shape[0]
    high = changed_ref[:, width : width + 1].astype(F32)
    low = changed_ref[:, width + 1 : width + 2].astype(F32)
    token = lax.broadcasted_iota(jnp.int32, (capacity, tokens), 1).astype(F32)
    chosen = jnp.where(token == high * F32(LANES) + low, F32(1.0), F32(0.0)).astype(BF16)
    here = mm(chosen, jnp.ones((capacity, LANES), BF16), FIRST_FIRST)[:, :1] > 0.5
    step = held.shape[2]
    copies = []
    for c in range(width // step):
        at = slice(c * step, (c + 1) * step)
        placed = mm(chosen, changed_ref[:, at], FIRST_FIRST)
        held[c] = jnp.where(here, placed, shifted_ref[:, at].astype(F32)).astype(BF16)
        copies.append(pltpu.make_async_copy(held.at[c], out_hbm.at[0, 0, :, pl.ds(c * step, step)], sems.at[c]))
        copies[-1].start()
    for c in copies:
        c.wait()


def shards(output_grads, gate_values, routing, saved_inputs, expert_weights):
    owners = lax.axis_size("expert")
    replicas = lax.axis_size("dp")
    others = replicas - 1
    capacity = saved_inputs.shape[4]
    incoming = output_grads[0, 0]
    tokens, width = incoming.shape
    part = width // replicas
    weights = expert_weights[0]
    hid = weights.shape[1]
    rows = owners * capacity
    top = routing.shape[3]
    out = jax.ShapeDtypeStruct
    hbm = pl.BlockSpec(memory_space=pltpu.HBM)
    saved = saved_inputs[0, 0, 0]

    shifted = to_previous(incoming)

    routed, picked, ids, *fars = run(
        route_body,
        "route",
        [out((capacity, width), BF16), out((capacity, width), BF16), out((capacity, LANES), BF16)]
        + [out((rows, part), BF16)] * others,
        [in_hbm(v) for v in (jnp.transpose(routing[0, 0]), jnp.transpose(gate_values[0, 0]), incoming, saved)],
        ROUTE_COST,
        in_specs=[hbm] * 4,
        scratch=[
            pltpu.VMEM((top, tokens), jnp.int32),
            pltpu.VMEM((top, tokens), F32),
            pltpu.VMEM((tokens, width), BF16),
            pltpu.SemaphoreType.DMA((3,)),
            pltpu.SemaphoreType.DMA((max(others, 1), owners)),
        ],
    )
    inner, outer = pairs_of(owners)
    distant = [to_pair(routed, j) for j in range(1, outer)]
    arrived = [to_sibling(routed)] if inner == 2 else []
    for block in distant:
        arrived.append(block)
        if inner == 2:
            arrived.append(to_sibling(block))
    far_inputs = [exchange(f, "dp", k + 1) for k, f in enumerate(fars)]

    slope, active, hidden, own_inputs = run(
        forward_body,
        "forward",
        [
            out((hid, rows), F32),
            out((hid, rows), F32),
            out((rows, hid), BF16),
            out((rows, part), BF16),
        ],
        [in_hbm(saved), weights],
        4 * rows * hid * width,
        in_specs=[hbm, pl.BlockSpec(memory_space=pltpu.VMEM)],
        scratch=[
            pltpu.VMEM((rows, width), BF16),
            pltpu.SemaphoreType.DMA((owners,)),
        ],
    )

    mine = outer * capacity
    kept, given, grads = run(
        functools.partial(backward_body, owners),
        "backward",
        [out((mine, width), BF16)] * 2 + [out((rows, 2 * hid), BF16)],
        [routed, *arrived, weights, slope, active, *far_inputs],
        6 * rows * hid * width,
    )
    if inner == 2:
        given = to_sibling(given)
    sums = run(
        functools.partial(pair_body, inner == 2),
        "pair_sums",
        [out((capacity, width), BF16)] * (outer - 1),
        [kept, given],
        0,
    )
    returned = [to_pair(v, j, back=True) for j, v in enumerate(sums, 1)]
    own_rows, *fars = run(
        functools.partial(pack_body, owners),
        "pack",
        [out((rows, part), BF16)] + [out((rows, part + 3 * hid), BF16)] * others,
        [routed, *arrived, hidden, grads, given],
        0,
    )
    far_rows = [exchange(f, "dp", k + 1) for k, f in enumerate(fars)]

    changed = run(
        functools.partial(return_body, inner == 2),
        "sum_returned",
        [out((capacity, width + LANES), BF16)],
        [picked, ids, kept, given, *returned],
        SUM_COST,
    )[0]
    next_changed = to_previous(changed)

    columns = min(part, 512)
    pieces = 3 * part // columns
    weight_grads = run(
        functools.partial(weight_body, others),
        "weight_grads",
        [out((1, 3, hid, part), BF16)],
        [hidden, grads, own_inputs, own_rows, *far_inputs, *far_rows],
        6 * rows * replicas * hid * part,
        out_specs=[hbm],
        scratch=[pltpu.VMEM((pieces, hid, columns), BF16), pltpu.SemaphoreType.DMA((pieces,))],
    )[0]

    step = min(width, 1024)
    passed_grads = run(
        merge_body,
        "merge",
        [out((1, 1, tokens, width), BF16)],
        [shifted, next_changed],
        2 * capacity * tokens * width,
        out_specs=[hbm],
        scratch=[pltpu.VMEM((width // step, tokens, step), BF16), pltpu.SemaphoreType.DMA((width // step,))],
    )[0]
    return (passed_grads, weight_grads)


def solution(mesh):
    placed = (
        P("dp", "pipe", "expert", None),
        P("dp", "pipe", "expert", None),
        P("dp", "pipe", "expert", None),
        P("dp", "pipe", None, None, None, None),
        P("pipe", None, "expert", None),
    )
    return jax.shard_map(
        shards,
        mesh=mesh,
        in_specs=placed,
        out_specs=(P("dp", "pipe", "expert", None), P("pipe", None, "expert", "dp")),
        check_vma=False,
    )
```

```python
import functools

import jax
import jax.numpy as jnp
from jax import lax
from jax.experimental import pallas as pl
from jax.experimental.pallas import tpu as pltpu
from jax.sharding import PartitionSpec as P

BF16 = jnp.bfloat16
F32 = jnp.float32
LANES = 128
VMEM_LIMIT = 20 * 2**20
SUM_COST = 0
ROUTE_COST = 10**10
LAST_LAST = (((1,), (1,)), ((), ()))
FIRST_FIRST = (((0,), (0,)), ((), ()))
ROWS_COLS = (((1,), (0,)), ((), ()))


def partner(index, step, count):
    if count & (count - 1) == 0:
        return index ^ step
    return (index + step) % count


def origin(index, step, count):
    if count & (count - 1) == 0:
        return index ^ step
    return (index - step) % count


def pairs_of(owners):
    inner = 2 if owners % 2 == 0 else 1
    return inner, owners // inner


def source(me, block, owners):
    inner, outer = pairs_of(owners)
    return origin(me // inner, block // inner, outer) * inner + (me % inner ^ block % inner)


def exchange(value, axis, step):
    count = lax.axis_size(axis)
    return lax.ppermute(value, axis, [(i, partner(i, step, count)) for i in range(count)])


def to_sibling(value):
    return lax.ppermute(value, "expert", [(i, i ^ 1) for i in range(lax.axis_size("expert"))])


def to_pair(value, step, back=False):
    owners = lax.axis_size("expert")
    inner, outer = pairs_of(owners)
    hops = [(i, partner(i // inner, step, outer) * inner + i % inner) for i in range(owners)]
    return lax.ppermute(value, "expert", [(j, i) for i, j in hops] if back else hops)


def to_previous(value):
    count = lax.axis_size("pipe")
    return lax.ppermute(value, "pipe", [(i, (i - 1) % count) for i in range(count)])


def mm(left, right, dims):
    return lax.dot_general(left, right, dims, preferred_element_type=F32)


def run(body, name, outs, inputs, flops, in_specs=None, out_specs=None, scratch=()):
    vmem = pl.BlockSpec(memory_space=pltpu.VMEM)
    moved = sum(v.size * v.dtype.itemsize for v in inputs)
    return pl.pallas_call(
        body,
        name=name,
        out_shape=outs,
        in_specs=in_specs or [vmem] * len(inputs),
        out_specs=out_specs or [vmem] * len(outs),
        scratch_shapes=scratch,
        compiler_params=pltpu.CompilerParams(vmem_limit_bytes=VMEM_LIMIT),
        cost_estimate=pl.CostEstimate(flops=flops, bytes_accessed=moved, transcendentals=0),
    )(*inputs)


def in_hbm(value):
    return pltpu.with_memory_space_constraint(value, pltpu.HBM)


def route_body(routing_hbm, gates_hbm, incoming_hbm, saved_hbm, *refs):
    others = lax.axis_size("dp") - 1
    owners = lax.axis_size("expert")
    inner, _ = pairs_of(owners)
    routed_ref, picked_ref, ids_ref, rows_ref = refs[:4]
    fars = refs[4 : 4 + others]
    routing_ref, gates_ref, incoming_ref, sems, far_sem = refs[4 + others :]
    capacity = routed_ref.shape[0]
    tokens, width = incoming_ref.shape
    me = lax.axis_index("expert")
    replica = lax.axis_index("dp")
    fetches = [
        pltpu.make_async_copy(routing_hbm, routing_ref, sems.at[0]),
        pltpu.make_async_copy(gates_hbm, gates_ref, sems.at[1]),
        pltpu.make_async_copy(incoming_hbm, incoming_ref, sems.at[2]),
    ]
    for f in fetches:
        f.start()
    copies = [
        pltpu.make_async_copy(
            saved_hbm.at[source(me, k, owners)], rows_ref.at[pl.ds(k * capacity, capacity)], far_sem.at[others, k]
        )
        for k in range(owners)
    ]
    for r in range(others):
        part = fars[r].shape[1]
        first = pl.multiple_of(partner(replica, r + 1, others + 1) * part, LANES)
        for j in range(owners // inner):
            copies.append(
                pltpu.make_async_copy(
                    saved_hbm.at[source(me, j * inner, owners), :, pl.ds(first, part)],
                    fars[r].at[pl.ds(j * capacity, capacity)],
                    far_sem.at[r, j],
                )
            )
    for c in copies:
        c.start()
    fetches[0].wait()
    fetches[1].wait()
    matches = routing_ref[...] == 0
    member = jnp.max(jnp.where(matches, F32(1.0), F32(0.0)), axis=0, keepdims=True)
    share = jnp.sum(jnp.where(matches, gates_ref[...], F32(0.0)), axis=0, keepdims=True)
    earlier = lax.broadcasted_iota(jnp.int32, (tokens, tokens), 0) < lax.broadcasted_iota(
        jnp.int32, (tokens, tokens), 1
    )
    spread = jnp.broadcast_to(member, (capacity, tokens))
    slot = mm(spread.astype(BF16), jnp.where(earlier, F32(1.0), F32(0.0)).astype(BF16), ROWS_COLS)
    wanted = lax.broadcasted_iota(jnp.int32, (capacity, tokens), 0).astype(F32)
    chosen = jnp.where((slot == wanted) & (spread > 0.5), F32(1.0), F32(0.0))
    weighting = jnp.sum(chosen * share, axis=1, keepdims=True)
    token = lax.broadcasted_iota(jnp.int32, (capacity, tokens), 1)
    filled = jnp.sum(chosen, axis=1, keepdims=True)
    high = jnp.sum(chosen * (token // LANES).astype(F32), axis=1, keepdims=True)
    low = jnp.sum(chosen * (token % LANES).astype(F32), axis=1, keepdims=True)
    high = jnp.where(filled > 0.5, high, F32(-1.0))
    lane = lax.broadcasted_iota(jnp.int32, (capacity, LANES), 1)
    ids_ref[...] = jnp.where(lane == 0, high, jnp.where(lane == 1, low, F32(0.0))).astype(BF16)
    fetches[2].wait()
    picked = mm(chosen.astype(BF16), incoming_ref[...], ROWS_COLS)
    routed_ref[...] = (picked * weighting).astype(BF16)
    picked_ref[...] = picked.astype(BF16)
    for c in copies:
        c.wait()


def forward_body(rows_ref, weights_ref, slope_ref, active_ref, hidden_ref):
    rows = rows_ref[...]
    gate_pre = mm(weights_ref[0], rows, LAST_LAST)
    up_pre = mm(weights_ref[1], rows, LAST_LAST)
    sigmoid_gate = jax.nn.sigmoid(gate_pre)
    activated = gate_pre * sigmoid_gate
    slope_ref[...] = up_pre * sigmoid_gate * (1.0 + gate_pre * (1.0 - sigmoid_gate))
    active_ref[...] = activated
    hidden_ref[...] = jnp.transpose(activated * up_pre).astype(BF16)


def backward_body(order, *refs):
    blocks = refs[:order]
    weights_ref, slope_ref, active_ref, hidden_ref = refs[order : order + 4]
    kept_ref, given_ref, grads_ref = refs[-3:]
    inner, outer = pairs_of(order)
    rows = jnp.concatenate([b[...] for b in blocks], axis=0)
    hidden_grad = mm(weights_ref[2], rows, LAST_LAST)
    gate_grad = jnp.transpose(hidden_grad * slope_ref[...]).astype(BF16)
    up_grad = jnp.transpose(hidden_grad * active_ref[...]).astype(BF16)
    capacity, width = blocks[0].shape
    step = 512
    for c in range(width // step):
        at = slice(c * step, (c + 1) * step)
        total = mm(gate_grad, weights_ref[0, :, at], ROWS_COLS) + mm(up_grad, weights_ref[1, :, at], ROWS_COLS)
        for k in range(order):
            into = kept_ref if k % inner == 0 else given_ref
            j = k // inner
            into[j * capacity : (j + 1) * capacity, at] = total[k * capacity : (k + 1) * capacity].astype(BF16)
    hid = weights_ref.shape[1]
    grads_ref[:, :hid] = gate_grad
    grads_ref[:, hid : 2 * hid] = up_grad
    grads_ref[:, 2 * hid :] = hidden_ref[...]


def pair_body(paired, others, kept_ref, given_ref, *refs):
    outs = refs[others:]
    capacity = outs[0].shape[0]
    for j, ref in enumerate(outs, 1):
        at = slice(j * capacity, (j + 1) * capacity)
        total = kept_ref[at].astype(F32)
        ref[...] = (total + given_ref[at].astype(F32) if paired else total).astype(BF16)


def pack_body(outer, *refs):
    blocks, fars = refs[:outer], refs[outer:]
    capacity = blocks[0].shape[0]
    part = fars[0].shape[1]
    replica = lax.axis_index("dp")
    for r, into in enumerate(fars, 1):
        first = pl.multiple_of(partner(replica, r, len(fars) + 1) * part, LANES)
        for j in range(outer):
            into[j * capacity : (j + 1) * capacity] = blocks[j][:, pl.ds(first, part)]


def return_body(paired, picked_ref, ids_ref, kept_ref, given_ref, *refs):
    returned, out_ref = refs[:-1], refs[-1]
    capacity, width = picked_ref.shape
    back = kept_ref[:capacity].astype(F32)
    if paired:
        back = back + given_ref[:capacity].astype(F32)
    for ref in returned:
        back = back + ref[...].astype(F32)
    out_ref[:, :width] = (picked_ref[...].astype(F32) + back).astype(BF16)
    out_ref[:, width:] = ids_ref[...]


def weight_body(others, owners, factors_ref, inputs_ref, *refs):
    inner, outer = pairs_of(owners)
    halves = others * inner
    blocks, refs = refs[:owners], refs[owners:]
    far_inputs, far_rows, far_factors = refs[:halves], refs[halves : 2 * halves], refs[2 * halves : 2 * halves + others]
    out_hbm, held, sems = refs[2 * halves + others :]
    capacity = blocks[0].shape[0]
    hid, part = out_hbm.shape[2:]
    columns = held.shape[2]
    replica = lax.axis_index("dp")
    left = [
        jnp.concatenate([f[:, i * hid : (i + 1) * hid] for f in (factors_ref, *far_factors)], axis=0) for i in range(3)
    ]

    def far(halves_of, at):
        return [
            halves_of[r * inner + i][j * capacity : (j + 1) * capacity, at]
            for r in range(others)
            for j in range(outer)
            for i in range(inner)
        ]

    copies = []
    for c in range(part // columns):
        at = slice(c * columns, (c + 1) * columns)
        own = pl.ds(pl.multiple_of(replica * part + c * columns, LANES), columns)
        inputs = jnp.concatenate([inputs_ref[:, own]] + far(far_inputs, at), axis=0)
        rows = jnp.concatenate([b[:, own] for b in blocks] + far(far_rows, at), axis=0)
        for i in range(3):
            n = len(copies)
            held[n] = mm(left[i], rows if i == 2 else inputs, FIRST_FIRST).astype(BF16)
            copies.append(pltpu.make_async_copy(held.at[n], out_hbm.at[0, i, :, pl.ds(c * columns, columns)], sems.at[n]))
            copies[-1].start()
    for c in copies:
        c.wait()


def merge_body(shifted_ref, changed_ref, out_hbm, held, sems):
    tokens, width = shifted_ref.shape
    capacity = changed_ref.shape[0]
    high = changed_ref[:, width : width + 1].astype(F32)
    low = changed_ref[:, width + 1 : width + 2].astype(F32)
    token = lax.broadcasted_iota(jnp.int32, (capacity, tokens), 1).astype(F32)
    chosen = jnp.where(token == high * F32(LANES) + low, F32(1.0), F32(0.0)).astype(BF16)
    here = mm(chosen, jnp.ones((capacity, LANES), BF16), FIRST_FIRST)[:, :1] > 0.5
    step = held.shape[2]
    copies = []
    for c in range(width // step):
        at = slice(c * step, (c + 1) * step)
        placed = mm(chosen, changed_ref[:, at], FIRST_FIRST)
        held[c] = jnp.where(here, placed, shifted_ref[:, at].astype(F32)).astype(BF16)
        copies.append(pltpu.make_async_copy(held.at[c], out_hbm.at[0, 0, :, pl.ds(c * step, step)], sems.at[c]))
        copies[-1].start()
    for c in copies:
        c.wait()


def shards(output_grads, gate_values, routing, saved_inputs, expert_weights):
    owners = lax.axis_size("expert")
    replicas = lax.axis_size("dp")
    others = replicas - 1
    capacity = saved_inputs.shape[4]
    incoming = output_grads[0, 0]
    tokens, width = incoming.shape
    part = width // replicas
    weights = expert_weights[0]
    hid = weights.shape[1]
    rows = owners * capacity
    top = routing.shape[3]
    inner, outer = pairs_of(owners)
    mine = outer * capacity
    out = jax.ShapeDtypeStruct
    hbm = pl.BlockSpec(memory_space=pltpu.HBM)
    saved = saved_inputs[0, 0, 0]

    shifted = to_previous(incoming)

    routed, picked, ids, own_inputs, *fars = run(
        route_body,
        "route",
        [out((capacity, width), BF16), out((capacity, width), BF16), out((capacity, LANES), BF16)]
        + [out((rows, width), BF16)]
        + [out((mine, part), BF16)] * others,
        [in_hbm(v) for v in (jnp.transpose(routing[0, 0]), jnp.transpose(gate_values[0, 0]), incoming, saved)],
        ROUTE_COST,
        in_specs=[hbm] * 4,
        scratch=[
            pltpu.VMEM((top, tokens), jnp.int32),
            pltpu.VMEM((top, tokens), F32),
            pltpu.VMEM((tokens, width), BF16),
            pltpu.SemaphoreType.DMA((3,)),
            pltpu.SemaphoreType.DMA((replicas, owners)),
        ],
    )
    distant = [to_pair(routed, j) for j in range(1, outer)]
    arrived = [to_sibling(routed)] if inner == 2 else []
    far_inputs = [exchange(f, "dp", k + 1) for k, f in enumerate(fars)]

    def both_halves(values):
        return [h for v in values for h in ((v, to_sibling(v)) if inner == 2 else (v,))]

    slope, active, hidden = run(
        forward_body,
        "forward",
        [out((hid, rows), F32), out((hid, rows), F32), out((rows, hid), BF16)],
        [own_inputs, weights],
        4 * rows * hid * width,
    )
    *distant, hidden = lax.optimization_barrier((*distant, hidden))
    for block in distant:
        arrived.append(block)
        if inner == 2:
            arrived.append(to_sibling(block))

    fars = run(
        functools.partial(pack_body, outer),
        "pack",
        [out((mine, part), BF16)] * others,
        [routed, *distant],
        0,
    )
    far_rows = both_halves([exchange(f, "dp", k + 1) for k, f in enumerate(fars)])
    far_inputs = both_halves(far_inputs)

    kept, given, grads = run(
        functools.partial(backward_body, owners),
        "backward",
        [out((mine, width), BF16)] * 2 + [out((rows, 3 * hid), BF16)],
        [routed, *arrived, weights, slope, active, hidden],
        6 * rows * hid * width,
    )
    if inner == 2:
        given = to_sibling(given)
    sums = run(
        functools.partial(pair_body, inner == 2, len(far_inputs)),
        "pair_sums",
        [out((capacity, width), BF16)] * (outer - 1),
        [kept, given, *far_inputs],
        0,
    )
    returned = [to_pair(v, j, back=True) for j, v in enumerate(sums, 1)]
    far_grads = [exchange(grads, "dp", k) for k in range(1, replicas)]

    changed = run(
        functools.partial(return_body, inner == 2),
        "sum_returned",
        [out((capacity, width + LANES), BF16)],
        [picked, ids, kept, given, *returned],
        SUM_COST,
    )[0]
    next_changed = to_previous(changed)

    columns = min(part, 512)
    pieces = 3 * part // columns
    weight_grads = run(
        functools.partial(weight_body, others, owners),
        "weight_grads",
        [out((1, 3, hid, part), BF16)],
        [grads, own_inputs, routed, *arrived, *far_inputs, *far_rows, *far_grads],
        6 * rows * replicas * hid * part,
        out_specs=[hbm],
        scratch=[pltpu.VMEM((pieces, hid, columns), BF16), pltpu.SemaphoreType.DMA((pieces,))],
    )[0]

    step = min(width, 1024)
    passed_grads = run(
        merge_body,
        "merge",
        [out((1, 1, tokens, width), BF16)],
        [shifted, next_changed],
        2 * capacity * tokens * width,
        out_specs=[hbm],
        scratch=[pltpu.VMEM((width // step, tokens, step), BF16), pltpu.SemaphoreType.DMA((width // step,))],
    )[0]
    return (passed_grads, weight_grads)


def solution(mesh):
    placed = (
        P("dp", "pipe", "expert", None),
        P("dp", "pipe", "expert", None),
        P("dp", "pipe", "expert", None),
        P("dp", "pipe", None, None, None, None),
        P("pipe", None, "expert", None),
    )
    return jax.shard_map(
        shards,
        mesh=mesh,
        in_specs=placed,
        out_specs=(P("dp", "pipe", "expert", None), P("pipe", None, "expert", "dp")),
        check_vma=False,
    )
```

```python
import functools

import jax
import jax.numpy as jnp
from jax import lax
from jax.experimental import pallas as pl
from jax.experimental.pallas import tpu as pltpu
from jax.sharding import PartitionSpec as P

BF16 = jnp.bfloat16
F32 = jnp.float32
LANES = 128
VMEM_LIMIT = 20 * 2**20
ROUTE_COST = 10**10
LAST_LAST = (((1,), (1,)), ((), ()))
FIRST_FIRST = (((0,), (0,)), ((), ()))
ROWS_COLS = (((1,), (0,)), ((), ()))


def partner(index, step, count):
    if count & (count - 1) == 0:
        return index ^ step
    return (index + step) % count


def origin(index, step, count):
    if count & (count - 1) == 0:
        return index ^ step
    return (index - step) % count


def pairs_of(owners):
    inner = 2 if owners % 2 == 0 else 1
    return inner, owners // inner


def source(me, block, owners):
    inner, outer = pairs_of(owners)
    return origin(me // inner, block // inner, outer) * inner + (me % inner ^ block % inner)


def exchange(value, axis, step):
    count = lax.axis_size(axis)
    return lax.ppermute(value, axis, [(i, partner(i, step, count)) for i in range(count)])


def to_sibling(value):
    return lax.ppermute(value, "expert", [(i, i ^ 1) for i in range(lax.axis_size("expert"))])


def to_pair(value, step, back=False):
    owners = lax.axis_size("expert")
    inner, outer = pairs_of(owners)
    hops = [(i, partner(i // inner, step, outer) * inner + i % inner) for i in range(owners)]
    return lax.ppermute(value, "expert", [(j, i) for i, j in hops] if back else hops)


def to_previous(value):
    count = lax.axis_size("pipe")
    return lax.ppermute(value, "pipe", [(i, (i - 1) % count) for i in range(count)])


def mm(left, right, dims):
    return lax.dot_general(left, right, dims, preferred_element_type=F32)


def run(body, name, outs, inputs, flops, in_specs=None, out_specs=None, scratch=(), aliases=None):
    vmem = pl.BlockSpec(memory_space=pltpu.VMEM)
    moved = sum(v.size * v.dtype.itemsize for v in inputs)
    return pl.pallas_call(
        body,
        name=name,
        out_shape=outs,
        in_specs=in_specs or [vmem] * len(inputs),
        out_specs=out_specs or [vmem] * len(outs),
        scratch_shapes=scratch,
        input_output_aliases=aliases or {},
        compiler_params=pltpu.CompilerParams(vmem_limit_bytes=VMEM_LIMIT),
        cost_estimate=pl.CostEstimate(flops=flops, bytes_accessed=moved, transcendentals=0),
    )(*inputs)


def in_hbm(value):
    return pltpu.with_memory_space_constraint(value, pltpu.HBM)


def earlier_count(flags):
    lanes = flags.shape[1]
    before = lax.broadcasted_iota(jnp.int32, (lanes, lanes), 0) < lax.broadcasted_iota(jnp.int32, (lanes, lanes), 1)
    return mm(flags.astype(BF16), jnp.where(before, F32(1.0), F32(0.0)).astype(BF16), ROWS_COLS)


def one_hot(wanted, rows, valid):
    number = lax.broadcasted_iota(jnp.int32, (rows, wanted.shape[1]), 0).astype(F32)
    return jnp.where((number == wanted[:1]) & (valid[:1] > 0.5), F32(1.0), F32(0.0))


def choose_late(routing, gates, capacity):
    tokens = routing.shape[1]
    matches = routing == 0
    member = jnp.max(jnp.where(matches, F32(1.0), F32(0.0)), axis=0, keepdims=True)
    share = jnp.sum(jnp.where(matches, gates, F32(0.0)), axis=0, keepdims=True)
    spread = jnp.broadcast_to(member, (capacity, tokens))
    slot = earlier_count(spread)
    members = jnp.sum(spread, axis=1, keepdims=True)
    rank = lax.broadcasted_iota(jnp.int32, (capacity, tokens), 1).astype(F32) - slot
    left = rank - F32(tokens - capacity)
    is_late = jnp.where((spread > 0.5) | (left >= 0.0), F32(1.0), F32(0.0))
    chosen = one_hot(jnp.where(spread > 0.5, slot, members + left), capacity, is_late)
    weighting = jnp.sum(chosen * share, axis=1, keepdims=True)
    return chosen, weighting, one_hot(rank, tokens - capacity, 1.0 - is_late)


def route_body(
    routing_hbm, gates_hbm, incoming_hbm, early_ref, routed_ref, picked_ref, ids_ref, routing_ref, gates_ref, incoming_ref, sems
):
    capacity, width = routed_ref.shape
    fetches = [
        pltpu.make_async_copy(routing_hbm, routing_ref, sems.at[0]),
        pltpu.make_async_copy(gates_hbm, gates_ref, sems.at[1]),
        pltpu.make_async_copy(incoming_hbm, incoming_ref, sems.at[2]),
    ]
    for f in fetches:
        f.start()
    for f in fetches[:2]:
        f.wait()
    chosen, weighting, kept = choose_late(routing_ref[...], gates_ref[...], capacity)
    both = jnp.concatenate([kept, chosen], axis=0).astype(BF16)
    early = early_ref.shape[0]
    fetches[2].wait()
    step = min(width, 1024)
    for c in range(width // step):
        at = slice(c * step, (c + 1) * step)
        sorted_rows = mm(both, incoming_ref[:, at], ROWS_COLS)
        early_ref[:, at] = sorted_rows[:early].astype(BF16)
        picked_ref[:, at] = sorted_rows[early:].astype(BF16)
        routed_ref[:, at] = (sorted_rows[early:] * weighting).astype(BF16)
    token = lax.broadcasted_iota(jnp.int32, chosen.shape, 1)
    high = jnp.sum(chosen * (token // LANES).astype(F32), axis=1, keepdims=True)
    low = jnp.sum(chosen * (token % LANES).astype(F32), axis=1, keepdims=True)
    lane = lax.broadcasted_iota(jnp.int32, ids_ref.shape, 1)
    ids_ref[...] = jnp.where(lane == 0, high, jnp.where(lane == 1, low, F32(0.0))).astype(BF16)


def forward_body(saved_ref, weights_ref, slope_ref, active_ref, hidden_ref, rows_ref, *fars):
    owners, capacity, _ = saved_ref.shape
    others = len(fars)
    inner, outer = pairs_of(owners)
    me = lax.axis_index("expert")
    replica = lax.axis_index("dp")
    for k in range(owners):
        rows_ref[k * capacity : (k + 1) * capacity] = saved_ref[source(me, k, owners)]
    for r in range(others):
        part = fars[r].shape[1]
        first = pl.multiple_of(partner(replica, r + 1, others + 1) * part, LANES)
        for j in range(outer):
            fars[r][j * capacity : (j + 1) * capacity] = saved_ref[source(me, j * inner, owners), :, pl.ds(first, part)]
    rows = rows_ref[...]
    gate_pre = mm(weights_ref[0], rows, LAST_LAST)
    up_pre = mm(weights_ref[1], rows, LAST_LAST)
    sigmoid_gate = jax.nn.sigmoid(gate_pre)
    activated = gate_pre * sigmoid_gate
    slope_ref[...] = up_pre * sigmoid_gate * (1.0 + gate_pre * (1.0 - sigmoid_gate))
    active_ref[...] = activated
    hidden_ref[...] = jnp.transpose(activated * up_pre).astype(BF16)


def backward_body(order, *refs):
    blocks = refs[:order]
    weights_ref, slope_ref, active_ref, hidden_ref = refs[order : order + 4]
    kept_ref, given_ref, grads_ref = refs[-3:]
    inner, outer = pairs_of(order)
    rows = jnp.concatenate([b[...] for b in blocks], axis=0)
    hidden_grad = mm(weights_ref[2], rows, LAST_LAST)
    gate_grad = jnp.transpose(hidden_grad * slope_ref[...]).astype(BF16)
    up_grad = jnp.transpose(hidden_grad * active_ref[...]).astype(BF16)
    capacity, width = blocks[0].shape
    step = 512
    for c in range(width // step):
        at = slice(c * step, (c + 1) * step)
        total = mm(gate_grad, weights_ref[0, :, at], ROWS_COLS) + mm(up_grad, weights_ref[1, :, at], ROWS_COLS)
        for k in range(order):
            into = kept_ref if k % inner == 0 else given_ref
            j = k // inner
            into[j * capacity : (j + 1) * capacity, at] = total[k * capacity : (k + 1) * capacity].astype(BF16)
    hid = weights_ref.shape[1]
    grads_ref[:, :hid] = gate_grad
    grads_ref[:, hid : 2 * hid] = up_grad
    grads_ref[:, 2 * hid :] = hidden_ref[...]


def pair_body(paired, others, kept_ref, given_ref, *refs):
    outs = refs[others:]
    capacity = outs[0].shape[0]
    for j, ref in enumerate(outs, 1):
        at = slice(j * capacity, (j + 1) * capacity)
        total = kept_ref[at].astype(F32)
        ref[...] = (total + given_ref[at].astype(F32) if paired else total).astype(BF16)


def pack_body(outer, *refs):
    blocks, fars = refs[:outer], refs[outer:]
    capacity = blocks[0].shape[0]
    part = fars[0].shape[1]
    replica = lax.axis_index("dp")
    for r, into in enumerate(fars, 1):
        first = pl.multiple_of(partner(replica, r, len(fars) + 1) * part, LANES)
        for j in range(outer):
            into[j * capacity : (j + 1) * capacity] = blocks[j][:, pl.ds(first, part)]


def return_body(paired, picked_ref, ids_ref, kept_ref, given_ref, *refs):
    returned, out_ref = refs[:-1], refs[-1]
    capacity, width = picked_ref.shape
    back = kept_ref[:capacity].astype(F32)
    if paired:
        back = back + given_ref[:capacity].astype(F32)
    for ref in returned:
        back = back + ref[...].astype(F32)
    out_ref[:, :width] = (picked_ref[...].astype(F32) + back).astype(BF16)
    out_ref[:, width:] = ids_ref[...]


def weight_body(others, owners, factors_ref, inputs_ref, *refs):
    inner, outer = pairs_of(owners)
    halves = others * inner
    blocks, refs = refs[:owners], refs[owners:]
    far_inputs, far_rows, far_factors = refs[:halves], refs[halves : 2 * halves], refs[2 * halves : 2 * halves + others]
    out_hbm, held, sems = refs[2 * halves + others :]
    capacity = blocks[0].shape[0]
    hid, part = out_hbm.shape[2:]
    columns = held.shape[2]
    replica = lax.axis_index("dp")
    left = [
        jnp.concatenate([f[:, i * hid : (i + 1) * hid] for f in (factors_ref, *far_factors)], axis=0) for i in range(3)
    ]

    def far(halves_of, at):
        return [
            halves_of[r * inner + i][j * capacity : (j + 1) * capacity, at]
            for r in range(others)
            for j in range(outer)
            for i in range(inner)
        ]

    copies = []
    for c in range(part // columns):
        at = slice(c * columns, (c + 1) * columns)
        own = pl.ds(pl.multiple_of(replica * part + c * columns, LANES), columns)
        inputs = jnp.concatenate([inputs_ref[:, own]] + far(far_inputs, at), axis=0)
        rows = jnp.concatenate([b[:, own] for b in blocks] + far(far_rows, at), axis=0)
        for i in range(3):
            n = len(copies)
            held[n] = mm(left[i], rows if i == 2 else inputs, FIRST_FIRST).astype(BF16)
            copies.append(pltpu.make_async_copy(held.at[n], out_hbm.at[0, i, :, pl.ds(c * columns, columns)], sems.at[n]))
            copies[-1].start()
    for c in copies:
        c.wait()


def merge_body(early_ref, changed_ref, out_hbm, held, sems):
    early, width = early_ref.shape
    capacity = changed_ref.shape[0]
    tokens = early + capacity
    high = changed_ref[:, width : width + 1].astype(F32)
    low = changed_ref[:, width + 1 : width + 2].astype(F32)
    token = lax.broadcasted_iota(jnp.int32, (capacity, tokens), 1).astype(F32)
    chosen = jnp.where(token == high * F32(LANES) + low, F32(1.0), F32(0.0))
    is_late = jnp.broadcast_to(jnp.sum(chosen, axis=0, keepdims=True), (capacity, tokens))
    kept = one_hot(token - earlier_count(is_late), early, 1.0 - is_late)
    both = jnp.concatenate([kept, chosen], axis=0).astype(BF16)
    step = held.shape[2]
    copies = []
    for c in range(width // step):
        at = slice(c * step, (c + 1) * step)
        rows = jnp.concatenate([early_ref[:, at], changed_ref[:, at]], axis=0)
        held[c] = mm(both, rows, FIRST_FIRST).astype(BF16)
        copies.append(pltpu.make_async_copy(held.at[c], out_hbm.at[0, 0, :, pl.ds(c * step, step)], sems.at[c]))
        copies[-1].start()
    for c in copies:
        c.wait()


def shards(output_grads, gate_values, routing, saved_inputs, expert_weights):
    owners = lax.axis_size("expert")
    replicas = lax.axis_size("dp")
    others = replicas - 1
    capacity = saved_inputs.shape[4]
    incoming = output_grads[0, 0]
    tokens, width = incoming.shape
    part = width // replicas
    weights = expert_weights[0]
    hid = weights.shape[1]
    rows = owners * capacity
    top = routing.shape[3]
    inner, outer = pairs_of(owners)
    mine = outer * capacity
    out = jax.ShapeDtypeStruct
    hbm = pl.BlockSpec(memory_space=pltpu.HBM)
    saved = saved_inputs[0, 0, 0]

    early = tokens - capacity
    early_rows, routed, picked, ids = run(
        route_body,
        "route",
        [
            out((early, width), BF16),
            out((capacity, width), BF16),
            out((capacity, width), BF16),
            out((capacity, LANES), BF16),
        ],
        [in_hbm(v) for v in (jnp.transpose(routing[0, 0]), jnp.transpose(gate_values[0, 0]), incoming)],
        ROUTE_COST,
        in_specs=[hbm] * 3,
        scratch=[
            pltpu.VMEM((top, tokens), jnp.int32),
            pltpu.VMEM((top, tokens), F32),
            pltpu.VMEM((tokens, width), BF16),
            pltpu.SemaphoreType.DMA((3,)),
        ],
    )
    shifted = to_previous(early_rows)
    distant = [to_pair(routed, j) for j in range(1, outer)]
    arrived = [to_sibling(routed)] if inner == 2 else []

    def both_halves(values):
        return [h for v in values for h in ((v, to_sibling(v)) if inner == 2 else (v,))]

    slope, active, hidden, own_inputs, *fars = run(
        forward_body,
        "forward",
        [out((hid, rows), F32), out((hid, rows), F32), out((rows, hid), BF16), out((rows, width), BF16)]
        + [out((mine, part), BF16)] * others,
        [saved, weights],
        4 * rows * hid * width,
    )
    far_inputs = [exchange(f, "dp", k + 1) for k, f in enumerate(fars)]
    *distant, hidden = lax.optimization_barrier((*distant, hidden))
    for block in distant:
        arrived.append(block)
        if inner == 2:
            arrived.append(to_sibling(block))

    fars = run(
        functools.partial(pack_body, outer),
        "pack",
        [out((mine, part), BF16)] * others,
        [routed, *distant],
        0,
    )
    far_rows = both_halves([exchange(f, "dp", k + 1) for k, f in enumerate(fars)])
    far_inputs = both_halves(far_inputs)

    kept, given, grads = run(
        functools.partial(backward_body, owners),
        "backward",
        [out((mine, width), BF16)] * 2 + [out((rows, 3 * hid), BF16)],
        [routed, *arrived, weights, slope, active, hidden],
        6 * rows * hid * width,
    )
    if inner == 2:
        given = to_sibling(given)
    sums = run(
        functools.partial(pair_body, inner == 2, len(far_inputs)),
        "pair_sums",
        [out((capacity, width), BF16)] * (outer - 1),
        [kept, given, *far_inputs],
        0,
    )
    returned = [to_pair(v, j, back=True) for j, v in enumerate(sums, 1)]
    far_grads = [exchange(grads, "dp", k) for k in range(1, replicas)]

    changed = run(
        functools.partial(return_body, inner == 2),
        "sum_returned",
        [out((capacity, width + LANES), BF16)],
        [picked, ids, kept, given, *returned],
        0,
    )[0]
    next_changed = to_previous(changed)

    columns = min(part, 512)
    pieces = 3 * part // columns
    weight_grads = run(
        functools.partial(weight_body, others, owners),
        "weight_grads",
        [out((1, 3, hid, part), BF16)],
        [grads, own_inputs, routed, *arrived, *far_inputs, *far_rows, *far_grads],
        6 * rows * replicas * hid * part,
        out_specs=[hbm],
        scratch=[pltpu.VMEM((pieces, hid, columns), BF16), pltpu.SemaphoreType.DMA((pieces,))],
    )[0]

    step = min(width, 1024)
    passed_grads = run(
        merge_body,
        "merge",
        [out((1, 1, tokens, width), BF16)],
        [shifted, next_changed],
        2 * capacity * tokens * width,
        out_specs=[hbm],
        scratch=[pltpu.VMEM((width // step, tokens, step), BF16), pltpu.SemaphoreType.DMA((width // step,))],
    )[0]
    return (passed_grads, weight_grads)


def solution(mesh):
    placed = (
        P("dp", "pipe", "expert", None),
        P("dp", "pipe", "expert", None),
        P("dp", "pipe", "expert", None),
        P("dp", "pipe", None, None, None, None),
        P("pipe", None, "expert", None),
    )
    return jax.shard_map(
        shards,
        mesh=mesh,
        in_specs=placed,
        out_specs=(P("dp", "pipe", "expert", None), P("pipe", None, "expert", "dp")),
        check_vma=False,
    )
```

```python
import functools

import jax
import jax.numpy as jnp
from jax import lax
from jax.experimental import pallas as pl
from jax.experimental.pallas import tpu as pltpu
from jax.sharding import PartitionSpec as P

BF16 = jnp.bfloat16
F32 = jnp.float32
LANES = 128
VMEM_LIMIT = 20 * 2**20
ROUTE_COST = 10**10
LAST_LAST = (((1,), (1,)), ((), ()))
FIRST_FIRST = (((0,), (0,)), ((), ()))
ROWS_COLS = (((1,), (0,)), ((), ()))


def partner(index, step, count):
    if count & (count - 1) == 0:
        return index ^ step
    return (index + step) % count


def origin(index, step, count):
    if count & (count - 1) == 0:
        return index ^ step
    return (index - step) % count


def pairs_of(owners):
    inner = 2 if owners % 2 == 0 else 1
    return inner, owners // inner


def source(me, block, owners):
    inner, outer = pairs_of(owners)
    return origin(me // inner, block // inner, outer) * inner + (me % inner ^ block % inner)


def exchange(value, axis, step):
    count = lax.axis_size(axis)
    return lax.ppermute(value, axis, [(i, partner(i, step, count)) for i in range(count)])


def to_sibling(value):
    return lax.ppermute(value, "expert", [(i, i ^ 1) for i in range(lax.axis_size("expert"))])


def to_pair(value, step, back=False):
    owners = lax.axis_size("expert")
    inner, outer = pairs_of(owners)
    hops = [(i, partner(i // inner, step, outer) * inner + i % inner) for i in range(owners)]
    return lax.ppermute(value, "expert", [(j, i) for i, j in hops] if back else hops)


def to_previous(value):
    count = lax.axis_size("pipe")
    return lax.ppermute(value, "pipe", [(i, (i - 1) % count) for i in range(count)])


def mm(left, right, dims):
    return lax.dot_general(left, right, dims, preferred_element_type=F32)


def run(body, name, outs, inputs, flops, in_specs=None, out_specs=None, scratch=(), aliases=None):
    vmem = pl.BlockSpec(memory_space=pltpu.VMEM)
    moved = sum(v.size * v.dtype.itemsize for v in inputs)
    return pl.pallas_call(
        body,
        name=name,
        out_shape=outs,
        in_specs=in_specs or [vmem] * len(inputs),
        out_specs=out_specs or [vmem] * len(outs),
        scratch_shapes=scratch,
        input_output_aliases=aliases or {},
        compiler_params=pltpu.CompilerParams(vmem_limit_bytes=VMEM_LIMIT),
        cost_estimate=pl.CostEstimate(flops=flops, bytes_accessed=moved, transcendentals=0),
    )(*inputs)


def in_hbm(value):
    return pltpu.with_memory_space_constraint(value, pltpu.HBM)


def earlier_count(flags):
    lanes = flags.shape[1]
    before = lax.broadcasted_iota(jnp.int32, (lanes, lanes), 0) < lax.broadcasted_iota(jnp.int32, (lanes, lanes), 1)
    return mm(flags.astype(BF16), jnp.where(before, F32(1.0), F32(0.0)).astype(BF16), ROWS_COLS)


def one_hot(wanted, rows):
    number = lax.broadcasted_iota(jnp.int32, (rows, wanted.shape[1]), 0).astype(F32)
    return jnp.where(number == wanted[:1], F32(1.0), F32(0.0))


def sorting(early_row, late_row, tokens, capacity):
    early = one_hot(early_row, tokens - capacity)
    return jnp.concatenate([early, one_hot(late_row, capacity)], axis=0).astype(BF16)


def choose_late(routing, gates, capacity):
    tokens = routing.shape[1]
    matches = routing == 0
    member = jnp.max(jnp.where(matches, F32(1.0), F32(0.0)), axis=0, keepdims=True)
    share = jnp.sum(jnp.where(matches, gates, F32(0.0)), axis=0, keepdims=True)
    spread = jnp.broadcast_to(member, (capacity, tokens))
    slot = earlier_count(spread)
    members = jnp.sum(spread, axis=1, keepdims=True)
    rank = lax.broadcasted_iota(jnp.int32, (capacity, tokens), 1).astype(F32) - slot
    left = rank - F32(tokens - capacity)
    is_late = jnp.where((spread > 0.5) | (left >= 0.0), F32(1.0), F32(0.0))
    late_row = jnp.where(is_late > 0.5, jnp.where(spread > 0.5, slot, members + left), F32(-1.0))
    weighting = jnp.sum(one_hot(late_row, capacity) * share, axis=1, keepdims=True)
    return jnp.where(is_late > 0.5, F32(-1.0), rank), late_row, weighting


def route_body(
    routing_hbm, gates_hbm, incoming_hbm, early_ref, routed_ref, picked_ref, ids_ref, routing_ref, gates_ref, incoming_ref, sems
):
    capacity, width = routed_ref.shape
    fetches = [
        pltpu.make_async_copy(routing_hbm, routing_ref, sems.at[0]),
        pltpu.make_async_copy(gates_hbm, gates_ref, sems.at[1]),
        pltpu.make_async_copy(incoming_hbm, incoming_ref, sems.at[2]),
    ]
    for f in fetches:
        f.start()
    for f in fetches[:2]:
        f.wait()
    early = early_ref.shape[0]
    early_row, late_row, weighting = choose_late(routing_ref[...], gates_ref[...], capacity)
    both = sorting(early_row, late_row, early + capacity, capacity)
    digits = [d for row in (early_row, late_row) for d in (row.astype(jnp.int32) >> 7, row.astype(jnp.int32) & 127)]
    number = lax.broadcasted_iota(jnp.int32, ids_ref.shape, 0)
    ids = digits[3]
    for i in range(3):
        ids = jnp.where(number == i, digits[i], ids)
    ids_ref[...] = ids.astype(F32).astype(BF16)
    fetches[2].wait()
    step = min(width, 1024)
    for c in range(width // step):
        at = slice(c * step, (c + 1) * step)
        sorted_rows = mm(both, incoming_ref[:, at], ROWS_COLS)
        early_ref[:, at] = sorted_rows[:early].astype(BF16)
        picked_ref[:, at] = sorted_rows[early:].astype(BF16)
        routed_ref[:, at] = (sorted_rows[early:] * weighting).astype(BF16)


def forward_body(saved_ref, weights_ref, slope_ref, active_ref, hidden_ref, rows_ref, *fars):
    owners, capacity, _ = saved_ref.shape
    others = len(fars)
    inner, outer = pairs_of(owners)
    me = lax.axis_index("expert")
    replica = lax.axis_index("dp")
    for k in range(owners):
        rows_ref[k * capacity : (k + 1) * capacity] = saved_ref[source(me, k, owners)]
    for r in range(others):
        part = fars[r].shape[1]
        first = pl.multiple_of(partner(replica, r + 1, others + 1) * part, LANES)
        for j in range(outer):
            fars[r][j * capacity : (j + 1) * capacity] = saved_ref[source(me, j * inner, owners), :, pl.ds(first, part)]
    rows = rows_ref[...]
    gate_pre = mm(weights_ref[0], rows, LAST_LAST)
    up_pre = mm(weights_ref[1], rows, LAST_LAST)
    sigmoid_gate = jax.nn.sigmoid(gate_pre)
    activated = gate_pre * sigmoid_gate
    slope_ref[...] = up_pre * sigmoid_gate * (1.0 + gate_pre * (1.0 - sigmoid_gate))
    active_ref[...] = activated
    hidden_ref[...] = jnp.transpose(activated * up_pre).astype(BF16)


def backward_body(order, *refs):
    blocks = refs[:order]
    weights_ref, slope_ref, active_ref, hidden_ref = refs[order : order + 4]
    kept_ref, grads_ref, *given = refs[order + 4 :]
    inner, outer = pairs_of(order)
    rows = jnp.concatenate([b[...] for b in blocks], axis=0)
    hidden_grad = mm(weights_ref[2], rows, LAST_LAST)
    gate_grad = jnp.transpose(hidden_grad * slope_ref[...]).astype(BF16)
    up_grad = jnp.transpose(hidden_grad * active_ref[...]).astype(BF16)
    capacity, width = blocks[0].shape
    step = 512
    for c in range(width // step):
        at = slice(c * step, (c + 1) * step)
        total = mm(gate_grad, weights_ref[0, :, at], ROWS_COLS) + mm(up_grad, weights_ref[1, :, at], ROWS_COLS)
        for k in range(order):
            j = k // inner
            block = total[k * capacity : (k + 1) * capacity].astype(BF16)
            if k % inner:
                given[j][:, at] = block
            else:
                kept_ref[j * capacity : (j + 1) * capacity, at] = block
    hid = weights_ref.shape[1]
    grads_ref[:, :hid] = gate_grad
    grads_ref[:, hid : 2 * hid] = up_grad
    grads_ref[:, 2 * hid :] = hidden_ref[...]


def pair_body(outer, paired, kept_ref, *refs):
    given, outs = refs[: outer - 1] if paired else (), refs[1 - outer :]
    capacity = outs[0].shape[0]
    for j, ref in enumerate(outs, 1):
        total = kept_ref[j * capacity : (j + 1) * capacity].astype(F32)
        if paired:
            total = total + given[j - 1][...].astype(F32)
        ref[...] = total.astype(BF16)


def pack_body(outer, *refs):
    blocks, fars = refs[:outer], refs[outer:]
    capacity = blocks[0].shape[0]
    part = fars[0].shape[1]
    replica = lax.axis_index("dp")
    for r, into in enumerate(fars, 1):
        first = pl.multiple_of(partner(replica, r, len(fars) + 1) * part, LANES)
        for j in range(outer):
            into[j * capacity : (j + 1) * capacity] = blocks[j][:, pl.ds(first, part)]


def return_body(picked_ref, ids_ref, kept_ref, *refs):
    returned, out_ref = refs[:-1], refs[-1]
    capacity, width = picked_ref.shape
    back = kept_ref[:capacity].astype(F32)
    for ref in returned:
        back = back + ref[...].astype(F32)
    out_ref[:, :width] = (picked_ref[...].astype(F32) + back).astype(BF16)
    out_ref[:, width:] = ids_ref[...]


def weight_body(others, owners, factors_ref, inputs_ref, *refs):
    inner, outer = pairs_of(owners)
    halves = others * inner
    blocks, refs = refs[:owners], refs[owners:]
    far_inputs, far_rows, far_factors = refs[:halves], refs[halves : 2 * halves], refs[2 * halves : 2 * halves + others]
    out_hbm, held, sems = refs[2 * halves + others :]
    capacity = blocks[0].shape[0]
    hid, part = out_hbm.shape[2:]
    columns = held.shape[2]
    replica = lax.axis_index("dp")
    left = [
        jnp.concatenate([f[:, i * hid : (i + 1) * hid] for f in (factors_ref, *far_factors)], axis=0) for i in range(3)
    ]

    def far(halves_of, at):
        return [
            halves_of[r * inner + i][j * capacity : (j + 1) * capacity, at]
            for r in range(others)
            for j in range(outer)
            for i in range(inner)
        ]

    copies = []
    for c in range(part // columns):
        at = slice(c * columns, (c + 1) * columns)
        own = pl.ds(pl.multiple_of(replica * part + c * columns, LANES), columns)
        inputs = jnp.concatenate([inputs_ref[:, own]] + far(far_inputs, at), axis=0)
        rows = jnp.concatenate([b[:, own] for b in blocks] + far(far_rows, at), axis=0)
        for i in range(3):
            n = len(copies)
            held[n] = mm(left[i], rows if i == 2 else inputs, FIRST_FIRST).astype(BF16)
            copies.append(pltpu.make_async_copy(held.at[n], out_hbm.at[0, i, :, pl.ds(c * columns, columns)], sems.at[n]))
            copies[-1].start()
    for c in copies:
        c.wait()


def merge_body(early_ref, changed_ref, out_hbm, held, sems):
    early, width = early_ref.shape
    capacity = changed_ref.shape[0]
    tokens = early + capacity
    digits = [changed_ref[:, width:][i : i + 1].astype(F32) for i in range(4)]
    both = sorting(digits[0] * 128.0 + digits[1], digits[2] * 128.0 + digits[3], tokens, capacity)
    step = held.shape[2]
    copies = []
    for c in range(width // step):
        at = slice(c * step, (c + 1) * step)
        rows = jnp.concatenate([early_ref[:, at], changed_ref[:, at]], axis=0)
        held[c] = mm(both, rows, FIRST_FIRST).astype(BF16)
        copies.append(pltpu.make_async_copy(held.at[c], out_hbm.at[0, 0, :, pl.ds(c * step, step)], sems.at[c]))
        copies[-1].start()
    for c in copies:
        c.wait()


def shards(output_grads, gate_values, routing, saved_inputs, expert_weights):
    owners = lax.axis_size("expert")
    replicas = lax.axis_size("dp")
    others = replicas - 1
    capacity = saved_inputs.shape[4]
    incoming = output_grads[0, 0]
    tokens, width = incoming.shape
    part = width // replicas
    weights = expert_weights[0]
    hid = weights.shape[1]
    rows = owners * capacity
    top = routing.shape[3]
    inner, outer = pairs_of(owners)
    mine = outer * capacity
    out = jax.ShapeDtypeStruct
    hbm = pl.BlockSpec(memory_space=pltpu.HBM)
    saved = saved_inputs[0, 0, 0]

    early = tokens - capacity
    early_rows, routed, picked, ids = run(
        route_body,
        "route",
        [
            out((early, width), BF16),
            out((capacity, width), BF16),
            out((capacity, width), BF16),
            out((capacity, tokens), BF16),
        ],
        [in_hbm(v) for v in (jnp.transpose(routing[0, 0]), jnp.transpose(gate_values[0, 0]), incoming)],
        ROUTE_COST,
        in_specs=[hbm] * 3,
        scratch=[
            pltpu.VMEM((top, tokens), jnp.int32),
            pltpu.VMEM((top, tokens), F32),
            pltpu.VMEM((tokens, width), BF16),
            pltpu.SemaphoreType.DMA((3,)),
        ],
    )
    shifted = to_previous(early_rows)
    distant = [to_pair(routed, j) for j in range(1, outer)]
    arrived = [to_sibling(routed)] if inner == 2 else []

    def both_halves(values):
        return [h for v in values for h in ((v, to_sibling(v)) if inner == 2 else (v,))]

    slope, active, hidden, own_inputs, *fars = run(
        forward_body,
        "forward",
        [out((hid, rows), F32), out((hid, rows), F32), out((rows, hid), BF16), out((rows, width), BF16)]
        + [out((mine, part), BF16)] * others,
        [saved, weights],
        4 * rows * hid * width,
    )
    far_inputs = [exchange(f, "dp", k + 1) for k, f in enumerate(fars)]
    *distant, hidden = lax.optimization_barrier((*distant, hidden))
    for block in distant:
        arrived.append(block)
        if inner == 2:
            arrived.append(to_sibling(block))

    fars = run(
        functools.partial(pack_body, outer),
        "pack",
        [out((mine, part), BF16)] * others,
        [routed, *distant],
        0,
    )
    far_rows = both_halves([exchange(f, "dp", k + 1) for k, f in enumerate(fars)])
    far_inputs = both_halves(far_inputs)

    kept, grads, *given = run(
        functools.partial(backward_body, owners),
        "backward",
        [out((mine, width), BF16), out((rows, 3 * hid), BF16)] + [out((capacity, width), BF16)] * ((inner - 1) * outer),
        [routed, *arrived, weights, slope, active, hidden],
        6 * rows * hid * width,
    )
    given = [to_sibling(v) for v in given]
    sums = run(
        functools.partial(pair_body, outer, inner == 2),
        "pair_sums",
        [out((capacity, width), BF16)] * (outer - 1),
        [kept, *given[1:], *far_inputs[::inner]],
        0,
    )
    returned = [to_pair(v, j, back=True) for j, v in enumerate(sums, 1)]
    far_grads = [exchange(grads, "dp", k) for k in range(1, replicas)]

    changed = run(
        return_body,
        "sum_returned",
        [out((capacity, width + tokens), BF16)],
        [picked, ids, kept, *given[:1], *returned],
        0,
    )[0]
    next_changed = to_previous(changed)

    columns = min(part, 512)
    pieces = 3 * part // columns
    weight_grads = run(
        functools.partial(weight_body, others, owners),
        "weight_grads",
        [out((1, 3, hid, part), BF16)],
        [grads, own_inputs, routed, *arrived, *far_inputs, *far_rows, *far_grads],
        6 * rows * replicas * hid * part,
        out_specs=[hbm],
        scratch=[pltpu.VMEM((pieces, hid, columns), BF16), pltpu.SemaphoreType.DMA((pieces,))],
    )[0]

    step = min(width, 1024)
    passed_grads = run(
        merge_body,
        "merge",
        [out((1, 1, tokens, width), BF16)],
        [shifted, next_changed],
        2 * capacity * tokens * width,
        out_specs=[hbm],
        scratch=[pltpu.VMEM((width // step, tokens, step), BF16), pltpu.SemaphoreType.DMA((width // step,))],
    )[0]
    return (passed_grads, weight_grads)


def solution(mesh):
    placed = (
        P("dp", "pipe", "expert", None),
        P("dp", "pipe", "expert", None),
        P("dp", "pipe", "expert", None),
        P("dp", "pipe", None, None, None, None),
        P("pipe", None, "expert", None),
    )
    return jax.shard_map(
        shards,
        mesh=mesh,
        in_specs=placed,
        out_specs=(P("dp", "pipe", "expert", None), P("pipe", None, "expert", "dp")),
        check_vma=False,
    )
```

```python
import functools

import jax
import jax.numpy as jnp
from jax import lax
from jax.experimental import pallas as pl
from jax.experimental.pallas import tpu as pltpu
from jax.sharding import PartitionSpec as P

BF16 = jnp.bfloat16
F32 = jnp.float32
LANES = 128
VMEM_LIMIT = 20 * 2**20
ROUTE_COST = 10**10
LAST_LAST = (((1,), (1,)), ((), ()))
FIRST_FIRST = (((0,), (0,)), ((), ()))
ROWS_COLS = (((1,), (0,)), ((), ()))


def partner(index, step, count):
    if count & (count - 1) == 0:
        return index ^ step
    return (index + step) % count


def origin(index, step, count):
    if count & (count - 1) == 0:
        return index ^ step
    return (index - step) % count


def pairs_of(owners):
    inner = 2 if owners % 2 == 0 else 1
    return inner, owners // inner


def source(me, block, owners):
    inner, outer = pairs_of(owners)
    return origin(me // inner, block // inner, outer) * inner + (me % inner ^ block % inner)


def exchange(value, axis, step):
    count = lax.axis_size(axis)
    return lax.ppermute(value, axis, [(i, partner(i, step, count)) for i in range(count)])


def to_sibling(value):
    return lax.ppermute(value, "expert", [(i, i ^ 1) for i in range(lax.axis_size("expert"))])


def to_pair(value, step, back=False):
    owners = lax.axis_size("expert")
    inner, outer = pairs_of(owners)
    hops = [(i, partner(i // inner, step, outer) * inner + i % inner) for i in range(owners)]
    return lax.ppermute(value, "expert", [(j, i) for i, j in hops] if back else hops)


def to_previous(value):
    count = lax.axis_size("pipe")
    return lax.ppermute(value, "pipe", [(i, (i - 1) % count) for i in range(count)])


def mm(left, right, dims):
    return lax.dot_general(left, right, dims, preferred_element_type=F32)


def run(body, name, outs, inputs, flops, moved=None, in_specs=None, out_specs=None, scratch=(), aliases=None):
    vmem = pl.BlockSpec(memory_space=pltpu.VMEM)
    if moved is None:
        moved = sum(v.size * v.dtype.itemsize for v in inputs)
    return pl.pallas_call(
        body,
        name=name,
        out_shape=outs,
        in_specs=in_specs or [vmem] * len(inputs),
        out_specs=out_specs or [vmem] * len(outs),
        scratch_shapes=scratch,
        input_output_aliases=aliases or {},
        compiler_params=pltpu.CompilerParams(vmem_limit_bytes=VMEM_LIMIT),
        cost_estimate=pl.CostEstimate(flops=flops, bytes_accessed=moved, transcendentals=0),
    )(*inputs)


def in_hbm(value):
    return pltpu.with_memory_space_constraint(value, pltpu.HBM)


def earlier_count(flags):
    lanes = flags.shape[1]
    before = lax.broadcasted_iota(jnp.int32, (lanes, lanes), 0) < lax.broadcasted_iota(jnp.int32, (lanes, lanes), 1)
    return mm(flags.astype(BF16), jnp.where(before, F32(1.0), F32(0.0)).astype(BF16), ROWS_COLS)


def one_hot(wanted, rows):
    number = lax.broadcasted_iota(jnp.int32, (rows, wanted.shape[1]), 0).astype(F32)
    return jnp.where(number == wanted[:1], F32(1.0), F32(0.0))


def sorting(early_row, late_row, tokens, capacity):
    early = one_hot(early_row, tokens - capacity)
    return jnp.concatenate([early, one_hot(late_row, capacity)], axis=0).astype(BF16)


def choose_late(routing, gates, capacity):
    tokens = routing.shape[1]
    matches = routing == 0
    member = jnp.max(jnp.where(matches, F32(1.0), F32(0.0)), axis=0, keepdims=True)
    share = jnp.sum(jnp.where(matches, gates, F32(0.0)), axis=0, keepdims=True)
    spread = jnp.broadcast_to(member, (capacity, tokens))
    slot = earlier_count(spread)
    members = jnp.sum(spread, axis=1, keepdims=True)
    rank = lax.broadcasted_iota(jnp.int32, (capacity, tokens), 1).astype(F32) - slot
    left = rank - F32(tokens - capacity)
    is_late = jnp.where((spread > 0.5) | (left >= 0.0), F32(1.0), F32(0.0))
    late_row = jnp.where(is_late > 0.5, jnp.where(spread > 0.5, slot, members + left), F32(-1.0))
    weighting = jnp.sum(one_hot(late_row, capacity) * share, axis=1, keepdims=True)
    return jnp.where(is_late > 0.5, F32(-1.0), rank), late_row, weighting


def store_late(both, weighting, incoming, picked_ref, routed_ref):
    picked = mm(both[-picked_ref.shape[0] :], incoming, ROWS_COLS)
    picked_ref[...] = picked.astype(BF16)
    routed_ref[...] = (picked * weighting).astype(BF16)


def route_body(
    routing_hbm,
    gates_hbm,
    incoming_hbm,
    early_ref,
    picked_ref,
    routed_ref,
    both_ref,
    weighting_ref,
    ids_ref,
    incoming_ref,
    routing_ref,
    gates_ref,
    sems,
):
    capacity, width = routed_ref.shape
    fetches = [
        pltpu.make_async_copy(routing_hbm, routing_ref, sems.at[0]),
        pltpu.make_async_copy(gates_hbm, gates_ref, sems.at[1]),
        pltpu.make_async_copy(incoming_hbm, incoming_ref, sems.at[2]),
    ]
    for f in fetches:
        f.start()
    for f in fetches[:2]:
        f.wait()
    early = early_ref.shape[0]
    early_row, late_row, weighting = choose_late(routing_ref[...], gates_ref[...], capacity)
    both = sorting(early_row, late_row, early + capacity, capacity)
    both_ref[...] = both
    weighting_ref[...] = jnp.broadcast_to(weighting, weighting_ref.shape)
    digits = [d for row in (early_row, late_row) for d in (row.astype(jnp.int32) >> 7, row.astype(jnp.int32) & 127)]
    number = lax.broadcasted_iota(jnp.int32, ids_ref.shape, 0)
    ids = digits[3]
    for i in range(3):
        ids = jnp.where(number == i, digits[i], ids)
    ids_ref[...] = ids.astype(F32).astype(BF16)
    fetches[2].wait()
    step = min(width, 1024)
    for c in range(width // step):
        at = slice(c * step, (c + 1) * step)
        early_ref[:, at] = mm(both[:early], incoming_ref[:, at], ROWS_COLS).astype(BF16)

    @pl.when(lax.axis_index("pipe") == 0)
    def _():
        store_late(both, weighting, incoming_ref[...], picked_ref, routed_ref)


def route_late_body(incoming_ref, both_ref, weighting_ref, _, __, picked_ref, routed_ref):
    @pl.when(lax.axis_index("pipe") > 0)
    def _():
        store_late(both_ref[...], weighting_ref[:, :1], incoming_ref[...], picked_ref, routed_ref)


def forward_body(saved_ref, weights_ref, slope_ref, active_ref, hidden_ref, rows_ref, *fars):
    owners, capacity, _ = saved_ref.shape
    others = len(fars)
    inner, outer = pairs_of(owners)
    me = lax.axis_index("expert")
    replica = lax.axis_index("dp")
    for k in range(owners):
        rows_ref[k * capacity : (k + 1) * capacity] = saved_ref[source(me, k, owners)]
    for r in range(others):
        part = fars[r].shape[1]
        first = pl.multiple_of(partner(replica, r + 1, others + 1) * part, LANES)
        for j in range(outer):
            fars[r][j * capacity : (j + 1) * capacity] = saved_ref[source(me, j * inner, owners), :, pl.ds(first, part)]
    rows = rows_ref[...]
    gate_pre = mm(weights_ref[0], rows, LAST_LAST)
    up_pre = mm(weights_ref[1], rows, LAST_LAST)
    sigmoid_gate = jax.nn.sigmoid(gate_pre)
    activated = gate_pre * sigmoid_gate
    slope_ref[...] = up_pre * sigmoid_gate * (1.0 + gate_pre * (1.0 - sigmoid_gate))
    active_ref[...] = activated
    hidden_ref[...] = jnp.transpose(activated * up_pre).astype(BF16)


def backward_body(order, *refs):
    blocks = refs[:order]
    weights_ref, slope_ref, active_ref, hidden_ref = refs[order : order + 4]
    kept_ref, grads_ref, *given = refs[order + 4 :]
    inner, outer = pairs_of(order)
    rows = jnp.concatenate([b[...] for b in blocks], axis=0)
    hidden_grad = mm(weights_ref[2], rows, LAST_LAST)
    gate_grad = jnp.transpose(hidden_grad * slope_ref[...]).astype(BF16)
    up_grad = jnp.transpose(hidden_grad * active_ref[...]).astype(BF16)
    capacity, width = blocks[0].shape
    step = 512
    for c in range(width // step):
        at = slice(c * step, (c + 1) * step)
        total = mm(gate_grad, weights_ref[0, :, at], ROWS_COLS) + mm(up_grad, weights_ref[1, :, at], ROWS_COLS)
        for k in range(order):
            j = k // inner
            block = total[k * capacity : (k + 1) * capacity].astype(BF16)
            if k % inner:
                given[j][:, at] = block
            else:
                kept_ref[j * capacity : (j + 1) * capacity, at] = block
    hid = weights_ref.shape[1]
    grads_ref[:, :hid] = gate_grad
    grads_ref[:, hid : 2 * hid] = up_grad
    grads_ref[:, 2 * hid :] = hidden_ref[...]


def pair_body(outer, paired, kept_ref, *refs):
    given, outs = refs[: outer - 1] if paired else (), refs[1 - outer :]
    capacity = outs[0].shape[0]
    for j, ref in enumerate(outs, 1):
        total = kept_ref[j * capacity : (j + 1) * capacity].astype(F32)
        if paired:
            total = total + given[j - 1][...].astype(F32)
        ref[...] = total.astype(BF16)


def pack_body(outer, *refs):
    blocks, fars = refs[:outer], refs[outer:]
    capacity = blocks[0].shape[0]
    part = fars[0].shape[1]
    replica = lax.axis_index("dp")
    for r, into in enumerate(fars, 1):
        first = pl.multiple_of(partner(replica, r, len(fars) + 1) * part, LANES)
        for j in range(outer):
            into[j * capacity : (j + 1) * capacity] = blocks[j][:, pl.ds(first, part)]


def return_body(picked_ref, ids_ref, kept_ref, *refs):
    returned, out_ref = refs[:-1], refs[-1]
    capacity, width = picked_ref.shape
    back = kept_ref[:capacity].astype(F32)
    for ref in returned:
        back = back + ref[...].astype(F32)
    out_ref[:, :width] = (picked_ref[...].astype(F32) + back).astype(BF16)
    out_ref[:, width:] = ids_ref[...]


def weight_body(others, owners, factors_ref, inputs_ref, *refs):
    inner, outer = pairs_of(owners)
    halves = others * inner
    blocks, refs = refs[:owners], refs[owners:]
    far_inputs, far_rows, far_factors = refs[:halves], refs[halves : 2 * halves], refs[2 * halves : 2 * halves + others]
    out_hbm, held, sems = refs[2 * halves + others :]
    capacity = blocks[0].shape[0]
    hid, part = out_hbm.shape[2:]
    columns = held.shape[2]
    replica = lax.axis_index("dp")
    left = [
        jnp.concatenate([f[:, i * hid : (i + 1) * hid] for f in (factors_ref, *far_factors)], axis=0) for i in range(3)
    ]

    def far(halves_of, at):
        return [
            halves_of[r * inner + i][j * capacity : (j + 1) * capacity, at]
            for r in range(others)
            for j in range(outer)
            for i in range(inner)
        ]

    copies = []
    for c in range(part // columns):
        at = slice(c * columns, (c + 1) * columns)
        own = pl.ds(pl.multiple_of(replica * part + c * columns, LANES), columns)
        inputs = jnp.concatenate([inputs_ref[:, own]] + far(far_inputs, at), axis=0)
        rows = jnp.concatenate([b[:, own] for b in blocks] + far(far_rows, at), axis=0)
        for i in range(3):
            n = len(copies)
            held[n] = mm(left[i], rows if i == 2 else inputs, FIRST_FIRST).astype(BF16)
            copies.append(pltpu.make_async_copy(held.at[n], out_hbm.at[0, i, :, pl.ds(c * columns, columns)], sems.at[n]))
            copies[-1].start()
    for c in copies:
        c.wait()


def merge_body(early_ref, changed_ref, out_hbm, held, sems):
    early, width = early_ref.shape
    capacity = changed_ref.shape[0]
    tokens = early + capacity
    digits = [changed_ref[:, width:][i : i + 1].astype(F32) for i in range(4)]
    both = sorting(digits[0] * 128.0 + digits[1], digits[2] * 128.0 + digits[3], tokens, capacity)
    step = held.shape[2]
    copies = []
    for c in range(width // step):
        at = slice(c * step, (c + 1) * step)
        rows = jnp.concatenate([early_ref[:, at], changed_ref[:, at]], axis=0)
        held[c] = mm(both, rows, FIRST_FIRST).astype(BF16)
        copies.append(pltpu.make_async_copy(held.at[c], out_hbm.at[0, 0, :, pl.ds(c * step, step)], sems.at[c]))
        copies[-1].start()
    for c in copies:
        c.wait()


def shards(output_grads, gate_values, routing, saved_inputs, expert_weights):
    owners = lax.axis_size("expert")
    replicas = lax.axis_size("dp")
    others = replicas - 1
    capacity = saved_inputs.shape[4]
    incoming = output_grads[0, 0]
    tokens, width = incoming.shape
    part = width // replicas
    weights = expert_weights[0]
    hid = weights.shape[1]
    rows = owners * capacity
    top = routing.shape[3]
    inner, outer = pairs_of(owners)
    mine = outer * capacity
    out = jax.ShapeDtypeStruct
    hbm = pl.BlockSpec(memory_space=pltpu.HBM)
    saved = saved_inputs[0, 0, 0]

    early = tokens - capacity
    late_outs = [out((capacity, width), BF16)] * 2
    early_rows, picked, routed, both, weighting, ids, incoming = run(
        route_body,
        "route",
        [
            out((early, width), BF16),
            *late_outs,
            out((tokens, tokens), BF16),
            out((capacity, LANES), F32),
            out((capacity, tokens), BF16),
            out((tokens, width), BF16),
        ],
        [in_hbm(v) for v in (jnp.transpose(routing[0, 0]), jnp.transpose(gate_values[0, 0]), incoming)],
        0,
        moved=0,
        in_specs=[hbm] * 3,
        scratch=[pltpu.VMEM((top, tokens), jnp.int32), pltpu.VMEM((top, tokens), F32), pltpu.SemaphoreType.DMA((3,))],
    )
    shifted = to_previous(early_rows)
    picked, routed = run(
        route_late_body,
        "route_late",
        late_outs,
        [incoming, both, weighting, picked, routed],
        ROUTE_COST,
        aliases={3: 0, 4: 1},
    )
    distant = [to_pair(routed, j) for j in range(1, outer)]
    arrived = [to_sibling(routed)] if inner == 2 else []

    def both_halves(values):
        return [h for v in values for h in ((v, to_sibling(v)) if inner == 2 else (v,))]

    slope, active, hidden, own_inputs, *fars = run(
        forward_body,
        "forward",
        [out((hid, rows), F32), out((hid, rows), F32), out((rows, hid), BF16), out((rows, width), BF16)]
        + [out((mine, part), BF16)] * others,
        [saved, weights],
        4 * rows * hid * width,
    )
    far_inputs = [exchange(f, "dp", k + 1) for k, f in enumerate(fars)]
    *distant, hidden = lax.optimization_barrier((*distant, hidden))
    for block in distant:
        arrived.append(block)
        if inner == 2:
            arrived.append(to_sibling(block))

    fars = run(
        functools.partial(pack_body, outer),
        "pack",
        [out((mine, part), BF16)] * others,
        [routed, *distant],
        0,
    )
    far_rows = both_halves([exchange(f, "dp", k + 1) for k, f in enumerate(fars)])
    far_inputs = both_halves(far_inputs)

    kept, grads, *given = run(
        functools.partial(backward_body, owners),
        "backward",
        [out((mine, width), BF16), out((rows, 3 * hid), BF16)] + [out((capacity, width), BF16)] * ((inner - 1) * outer),
        [routed, *arrived, weights, slope, active, hidden],
        6 * rows * hid * width,
    )
    given = [to_sibling(v) for v in given]
    sums = run(
        functools.partial(pair_body, outer, inner == 2),
        "pair_sums",
        [out((capacity, width), BF16)] * (outer - 1),
        [kept, *given[1:], *far_inputs[::inner]],
        0,
    )
    returned = [to_pair(v, j, back=True) for j, v in enumerate(sums, 1)]
    far_grads = [exchange(grads, "dp", k) for k in range(1, replicas)]

    changed = run(
        return_body,
        "sum_returned",
        [out((capacity, width + tokens), BF16)],
        [picked, ids, kept, *given[:1], *returned],
        0,
    )[0]
    next_changed = to_previous(changed)

    columns = min(part, 512)
    pieces = 3 * part // columns
    weight_grads = run(
        functools.partial(weight_body, others, owners),
        "weight_grads",
        [out((1, 3, hid, part), BF16)],
        [grads, own_inputs, routed, *arrived, *far_inputs, *far_rows, *far_grads],
        6 * rows * replicas * hid * part,
        out_specs=[hbm],
        scratch=[pltpu.VMEM((pieces, hid, columns), BF16), pltpu.SemaphoreType.DMA((pieces,))],
    )[0]

    step = min(width, 1024)
    passed_grads = run(
        merge_body,
        "merge",
        [out((1, 1, tokens, width), BF16)],
        [shifted, next_changed],
        2 * capacity * tokens * width,
        out_specs=[hbm],
        scratch=[pltpu.VMEM((width // step, tokens, step), BF16), pltpu.SemaphoreType.DMA((width // step,))],
    )[0]
    return (passed_grads, weight_grads)


def solution(mesh):
    placed = (
        P("dp", "pipe", "expert", None),
        P("dp", "pipe", "expert", None),
        P("dp", "pipe", "expert", None),
        P("dp", "pipe", None, None, None, None),
        P("pipe", None, "expert", None),
    )
    return jax.shard_map(
        shards,
        mesh=mesh,
        in_specs=placed,
        out_specs=(P("dp", "pipe", "expert", None), P("pipe", None, "expert", "dp")),
        check_vma=False,
    )
```

```python
import functools

import jax
import jax.numpy as jnp
from jax import lax
from jax.experimental import pallas as pl
from jax.experimental.pallas import tpu as pltpu
from jax.sharding import PartitionSpec as P

BF16 = jnp.bfloat16
F32 = jnp.float32
LANES = 128
VMEM_LIMIT = 20 * 2**20
ROUTE_COST = 10**10
LAST_LAST = (((1,), (1,)), ((), ()))
FIRST_FIRST = (((0,), (0,)), ((), ()))
ROWS_COLS = (((1,), (0,)), ((), ()))


def partner(index, step, count):
    if count & (count - 1) == 0:
        return index ^ step
    return (index + step) % count


def origin(index, step, count):
    if count & (count - 1) == 0:
        return index ^ step
    return (index - step) % count


def pairs_of(owners):
    inner = 2 if owners % 2 == 0 else 1
    return inner, owners // inner


def source(me, block, owners):
    inner, outer = pairs_of(owners)
    return origin(me // inner, block // inner, outer) * inner + (me % inner ^ block % inner)


def exchange(value, axis, step):
    count = lax.axis_size(axis)
    return lax.ppermute(value, axis, [(i, partner(i, step, count)) for i in range(count)])


def to_sibling(value):
    return lax.ppermute(value, "expert", [(i, i ^ 1) for i in range(lax.axis_size("expert"))])


def to_pair(value, step, back=False):
    owners = lax.axis_size("expert")
    inner, outer = pairs_of(owners)
    hops = [(i, partner(i // inner, step, outer) * inner + i % inner) for i in range(owners)]
    return lax.ppermute(value, "expert", [(j, i) for i, j in hops] if back else hops)


def to_previous(value):
    count = lax.axis_size("pipe")
    return lax.ppermute(value, "pipe", [(i, (i - 1) % count) for i in range(count)])


def mm(left, right, dims):
    return lax.dot_general(left, right, dims, preferred_element_type=F32)


def run(body, name, outs, inputs, flops, moved=None, in_specs=None, out_specs=None, scratch=(), aliases=None):
    vmem = pl.BlockSpec(memory_space=pltpu.VMEM)
    if moved is None:
        moved = sum(v.size * v.dtype.itemsize for v in inputs)
    return pl.pallas_call(
        body,
        name=name,
        out_shape=outs,
        in_specs=in_specs or [vmem] * len(inputs),
        out_specs=out_specs or [vmem] * len(outs),
        scratch_shapes=scratch,
        input_output_aliases=aliases or {},
        compiler_params=pltpu.CompilerParams(vmem_limit_bytes=VMEM_LIMIT),
        cost_estimate=pl.CostEstimate(flops=flops, bytes_accessed=moved, transcendentals=0),
    )(*inputs)


def in_hbm(value):
    return pltpu.with_memory_space_constraint(value, pltpu.HBM)


def earlier_count(flags):
    lanes = flags.shape[1]
    before = lax.broadcasted_iota(jnp.int32, (lanes, lanes), 0) < lax.broadcasted_iota(jnp.int32, (lanes, lanes), 1)
    return mm(flags.astype(BF16), jnp.where(before, F32(1.0), F32(0.0)).astype(BF16), ROWS_COLS)


def one_hot(wanted, rows):
    number = lax.broadcasted_iota(jnp.int32, (rows, wanted.shape[1]), 0).astype(F32)
    return jnp.where(number == wanted[:1], F32(1.0), F32(0.0))


def sorting(early_row, late_row, tokens, capacity):
    early = one_hot(early_row, tokens - capacity)
    return jnp.concatenate([early, one_hot(late_row, capacity)], axis=0).astype(BF16)


def choose_late(routing, gates, capacity):
    tokens = routing.shape[1]
    matches = routing == 0
    member = jnp.max(jnp.where(matches, F32(1.0), F32(0.0)), axis=0, keepdims=True)
    share = jnp.sum(jnp.where(matches, gates, F32(0.0)), axis=0, keepdims=True)
    spread = jnp.broadcast_to(member, (capacity, tokens))
    slot = earlier_count(spread)
    members = jnp.sum(spread, axis=1, keepdims=True)
    rank = lax.broadcasted_iota(jnp.int32, (capacity, tokens), 1).astype(F32) - slot
    left = rank - F32(tokens - capacity)
    is_late = jnp.where((spread > 0.5) | (left >= 0.0), F32(1.0), F32(0.0))
    late_row = jnp.where(is_late > 0.5, jnp.where(spread > 0.5, slot, members + left), F32(-1.0))
    weighting = jnp.sum(one_hot(late_row, capacity) * share, axis=1, keepdims=True)
    return jnp.where(is_late > 0.5, F32(-1.0), rank), late_row, weighting


def store_late(both, weighting, incoming, picked_ref, routed_ref):
    picked = mm(both[-picked_ref.shape[0] :], incoming, ROWS_COLS)
    picked_ref[...] = picked.astype(BF16)
    routed_ref[...] = (picked * weighting).astype(BF16)


def route_body(
    routing_hbm,
    gates_hbm,
    incoming_hbm,
    early_ref,
    picked_ref,
    routed_ref,
    both_ref,
    weighting_ref,
    ids_ref,
    incoming_ref,
    routing_ref,
    gates_ref,
    sems,
):
    capacity, width = routed_ref.shape
    fetches = [
        pltpu.make_async_copy(routing_hbm, routing_ref, sems.at[0]),
        pltpu.make_async_copy(gates_hbm, gates_ref, sems.at[1]),
        pltpu.make_async_copy(incoming_hbm, incoming_ref, sems.at[2]),
    ]
    for f in reversed(fetches):
        f.start()
    for f in fetches[:2]:
        f.wait()
    early = early_ref.shape[0]
    early_row, late_row, weighting = choose_late(routing_ref[...], gates_ref[...], capacity)
    both = sorting(early_row, late_row, early + capacity, capacity)
    both_ref[...] = both
    weighting_ref[...] = jnp.broadcast_to(weighting, weighting_ref.shape)
    digits = [d for row in (early_row, late_row) for d in (row.astype(jnp.int32) >> 7, row.astype(jnp.int32) & 127)]
    number = lax.broadcasted_iota(jnp.int32, ids_ref.shape, 0)
    ids = digits[3]
    for i in range(3):
        ids = jnp.where(number == i, digits[i], ids)
    ids_ref[...] = ids.astype(F32).astype(BF16)
    fetches[2].wait()
    step = min(width, 1024)
    for c in range(width // step):
        at = slice(c * step, (c + 1) * step)
        early_ref[:, at] = mm(both[:early], incoming_ref[:, at], ROWS_COLS).astype(BF16)

    @pl.when(lax.axis_index("pipe") == 0)
    def _():
        store_late(both, weighting, incoming_ref[...], picked_ref, routed_ref)


def route_late_body(incoming_ref, both_ref, weighting_ref, _, __, picked_ref, routed_ref):
    @pl.when(lax.axis_index("pipe") > 0)
    def _():
        store_late(both_ref[...], weighting_ref[:, :1], incoming_ref[...], picked_ref, routed_ref)


def forward_body(saved_ref, weights_ref, slope_ref, active_ref, hidden_ref, rows_ref, *fars):
    owners, capacity, _ = saved_ref.shape
    others = len(fars)
    inner, outer = pairs_of(owners)
    me = lax.axis_index("expert")
    replica = lax.axis_index("dp")
    for k in range(owners):
        rows_ref[k * capacity : (k + 1) * capacity] = saved_ref[source(me, k, owners)]
    for r in range(others):
        part = fars[r].shape[1]
        first = pl.multiple_of(partner(replica, r + 1, others + 1) * part, LANES)
        for j in range(outer):
            fars[r][j * capacity : (j + 1) * capacity] = saved_ref[source(me, j * inner, owners), :, pl.ds(first, part)]
    rows = rows_ref[...]
    gate_pre = mm(weights_ref[0], rows, LAST_LAST)
    up_pre = mm(weights_ref[1], rows, LAST_LAST)
    sigmoid_gate = jax.nn.sigmoid(gate_pre)
    activated = gate_pre * sigmoid_gate
    slope_ref[...] = up_pre * sigmoid_gate * (1.0 + gate_pre * (1.0 - sigmoid_gate))
    active_ref[...] = activated
    hidden_ref[...] = jnp.transpose(activated * up_pre).astype(BF16)


def backward_body(order, *refs):
    blocks = refs[:order]
    weights_ref, slope_ref, active_ref, hidden_ref = refs[order : order + 4]
    kept_ref, grads_ref, *given = refs[order + 4 :]
    inner, outer = pairs_of(order)
    rows = jnp.concatenate([b[...] for b in blocks], axis=0)
    hidden_grad = mm(weights_ref[2], rows, LAST_LAST)
    gate_grad = jnp.transpose(hidden_grad * slope_ref[...]).astype(BF16)
    up_grad = jnp.transpose(hidden_grad * active_ref[...]).astype(BF16)
    capacity, width = blocks[0].shape
    step = 512
    for c in range(width // step):
        at = slice(c * step, (c + 1) * step)
        total = mm(gate_grad, weights_ref[0, :, at], ROWS_COLS) + mm(up_grad, weights_ref[1, :, at], ROWS_COLS)
        for k in range(order):
            j = k // inner
            block = total[k * capacity : (k + 1) * capacity].astype(BF16)
            if k % inner:
                given[j][:, at] = block
            else:
                kept_ref[j * capacity : (j + 1) * capacity, at] = block
    hid = weights_ref.shape[1]
    grads_ref[:, :hid] = gate_grad
    grads_ref[:, hid : 2 * hid] = up_grad
    grads_ref[:, 2 * hid :] = hidden_ref[...]


def pair_body(outer, paired, kept_ref, *refs):
    given, outs = refs[: outer - 1] if paired else (), refs[1 - outer :]
    capacity = outs[0].shape[0]
    for j, ref in enumerate(outs, 1):
        total = kept_ref[j * capacity : (j + 1) * capacity].astype(F32)
        if paired:
            total = total + given[j - 1][...].astype(F32)
        ref[...] = total.astype(BF16)


def pack_body(outer, *refs):
    blocks, fars = refs[:outer], refs[outer:]
    capacity = blocks[0].shape[0]
    part = fars[0].shape[1]
    replica = lax.axis_index("dp")
    for r, into in enumerate(fars, 1):
        first = pl.multiple_of(partner(replica, r, len(fars) + 1) * part, LANES)
        for j in range(outer):
            into[j * capacity : (j + 1) * capacity] = blocks[j][:, pl.ds(first, part)]


def return_body(picked_ref, ids_ref, kept_ref, *refs):
    returned, out_ref = refs[:-1], refs[-1]
    capacity, width = picked_ref.shape
    back = kept_ref[:capacity].astype(F32)
    for ref in returned:
        back = back + ref[...].astype(F32)
    out_ref[:, :width] = (picked_ref[...].astype(F32) + back).astype(BF16)
    out_ref[:, width:] = ids_ref[...]


def weight_body(others, owners, factors_ref, inputs_ref, *refs):
    inner, outer = pairs_of(owners)
    halves = others * inner
    blocks, refs = refs[:owners], refs[owners:]
    far_inputs, far_rows, far_factors = refs[:halves], refs[halves : 2 * halves], refs[2 * halves : 2 * halves + others]
    out_hbm, held, sems = refs[2 * halves + others :]
    capacity = blocks[0].shape[0]
    hid, part = out_hbm.shape[2:]
    columns = held.shape[2]
    replica = lax.axis_index("dp")
    left = [
        jnp.concatenate([f[:, i * hid : (i + 1) * hid] for f in (factors_ref, *far_factors)], axis=0) for i in range(3)
    ]

    def far(halves_of, at):
        return [
            halves_of[r * inner + i][j * capacity : (j + 1) * capacity, at]
            for r in range(others)
            for j in range(outer)
            for i in range(inner)
        ]

    copies = []
    for c in range(part // columns):
        at = slice(c * columns, (c + 1) * columns)
        own = pl.ds(pl.multiple_of(replica * part + c * columns, LANES), columns)
        inputs = jnp.concatenate([inputs_ref[:, own]] + far(far_inputs, at), axis=0)
        rows = jnp.concatenate([b[:, own] for b in blocks] + far(far_rows, at), axis=0)
        for i in range(3):
            n = len(copies)
            held[n] = mm(left[i], rows if i == 2 else inputs, FIRST_FIRST).astype(BF16)
            copies.append(pltpu.make_async_copy(held.at[n], out_hbm.at[0, i, :, pl.ds(c * columns, columns)], sems.at[n]))
            copies[-1].start()
    for c in copies:
        c.wait()


def merge_body(early_ref, changed_ref, out_hbm, held, sems):
    early, width = early_ref.shape
    capacity = changed_ref.shape[0]
    tokens = early + capacity
    digits = [changed_ref[:, width:][i : i + 1].astype(F32) for i in range(4)]
    both = sorting(digits[0] * 128.0 + digits[1], digits[2] * 128.0 + digits[3], tokens, capacity)
    step = held.shape[2]
    copies = []
    for c in range(width // step):
        at = slice(c * step, (c + 1) * step)
        rows = jnp.concatenate([early_ref[:, at], changed_ref[:, at]], axis=0)
        held[c] = mm(both, rows, FIRST_FIRST).astype(BF16)
        copies.append(pltpu.make_async_copy(held.at[c], out_hbm.at[0, 0, :, pl.ds(c * step, step)], sems.at[c]))
        copies[-1].start()
    for c in copies:
        c.wait()


def shards(output_grads, gate_values, routing, saved_inputs, expert_weights):
    owners = lax.axis_size("expert")
    replicas = lax.axis_size("dp")
    others = replicas - 1
    capacity = saved_inputs.shape[4]
    incoming = output_grads[0, 0]
    tokens, width = incoming.shape
    part = width // replicas
    weights = expert_weights[0]
    hid = weights.shape[1]
    rows = owners * capacity
    top = routing.shape[3]
    inner, outer = pairs_of(owners)
    mine = outer * capacity
    out = jax.ShapeDtypeStruct
    hbm = pl.BlockSpec(memory_space=pltpu.HBM)
    saved = saved_inputs[0, 0, 0]

    early = tokens - capacity
    late_outs = [out((capacity, width), BF16)] * 2
    early_rows, picked, routed, both, weighting, ids, incoming = run(
        route_body,
        "route",
        [
            out((early, width), BF16),
            *late_outs,
            out((tokens, tokens), BF16),
            out((capacity, LANES), F32),
            out((capacity, tokens), BF16),
            out((tokens, width), BF16),
        ],
        [in_hbm(v) for v in (jnp.transpose(routing[0, 0]), jnp.transpose(gate_values[0, 0]), incoming)],
        0,
        moved=0,
        in_specs=[hbm] * 3,
        scratch=[pltpu.VMEM((top, tokens), jnp.int32), pltpu.VMEM((top, tokens), F32), pltpu.SemaphoreType.DMA((3,))],
    )
    shifted = to_previous(early_rows)
    picked, routed = run(
        route_late_body,
        "route_late",
        late_outs,
        [incoming, both, weighting, picked, routed],
        ROUTE_COST,
        aliases={3: 0, 4: 1},
    )
    distant = [to_pair(routed, j) for j in range(1, outer)]
    arrived = [to_sibling(routed)] if inner == 2 else []

    def both_halves(values):
        return [h for v in values for h in ((v, to_sibling(v)) if inner == 2 else (v,))]

    slope, active, hidden, own_inputs, *fars = run(
        forward_body,
        "forward",
        [out((hid, rows), F32), out((hid, rows), F32), out((rows, hid), BF16), out((rows, width), BF16)]
        + [out((mine, part), BF16)] * others,
        [saved, weights],
        4 * rows * hid * width,
    )
    far_inputs = [exchange(f, "dp", k + 1) for k, f in enumerate(fars)]
    *distant, hidden = lax.optimization_barrier((*distant, hidden))
    for block in distant:
        arrived.append(block)
        if inner == 2:
            arrived.append(to_sibling(block))

    fars = run(
        functools.partial(pack_body, outer),
        "pack",
        [out((mine, part), BF16)] * others,
        [routed, *distant],
        0,
    )
    far_rows = both_halves([exchange(f, "dp", k + 1) for k, f in enumerate(fars)])
    far_inputs = both_halves(far_inputs)

    kept, grads, *given = run(
        functools.partial(backward_body, owners),
        "backward",
        [out((mine, width), BF16), out((rows, 3 * hid), BF16)] + [out((capacity, width), BF16)] * ((inner - 1) * outer),
        [routed, *arrived, weights, slope, active, hidden],
        6 * rows * hid * width,
    )
    given = [to_sibling(v) for v in given]
    sums = run(
        functools.partial(pair_body, outer, inner == 2),
        "pair_sums",
        [out((capacity, width), BF16)] * (outer - 1),
        [kept, *given[1:], *far_inputs[::inner]],
        0,
    )
    returned = [to_pair(v, j, back=True) for j, v in enumerate(sums, 1)]
    far_grads = [exchange(grads, "dp", k) for k in range(1, replicas)]

    changed = run(
        return_body,
        "sum_returned",
        [out((capacity, width + tokens), BF16)],
        [picked, ids, kept, *given[:1], *returned],
        0,
    )[0]
    next_changed = to_previous(changed)

    columns = min(part, 512)
    pieces = 3 * part // columns
    weight_grads = run(
        functools.partial(weight_body, others, owners),
        "weight_grads",
        [out((1, 3, hid, part), BF16)],
        [grads, own_inputs, routed, *arrived, *far_inputs, *far_rows, *far_grads],
        6 * rows * replicas * hid * part,
        out_specs=[hbm],
        scratch=[pltpu.VMEM((pieces, hid, columns), BF16), pltpu.SemaphoreType.DMA((pieces,))],
    )[0]

    step = min(width, 1024)
    passed_grads = run(
        merge_body,
        "merge",
        [out((1, 1, tokens, width), BF16)],
        [shifted, next_changed],
        2 * capacity * tokens * width,
        out_specs=[hbm],
        scratch=[pltpu.VMEM((width // step, tokens, step), BF16), pltpu.SemaphoreType.DMA((width // step,))],
    )[0]
    return (passed_grads, weight_grads)


def solution(mesh):
    placed = (
        P("dp", "pipe", "expert", None),
        P("dp", "pipe", "expert", None),
        P("dp", "pipe", "expert", None),
        P("dp", "pipe", None, None, None, None),
        P("pipe", None, "expert", None),
    )
    return jax.shard_map(
        shards,
        mesh=mesh,
        in_specs=placed,
        out_specs=(P("dp", "pipe", "expert", None), P("pipe", None, "expert", "dp")),
        check_vma=False,
    )
```

```python
import functools

import jax
import jax.numpy as jnp
from jax import lax
from jax.experimental import pallas as pl
from jax.experimental.pallas import tpu as pltpu
from jax.sharding import PartitionSpec as P

BF16 = jnp.bfloat16
F32 = jnp.float32
LANES = 128
VMEM_LIMIT = 12 * 2**20
ROUTE_COST = 10**10
LAST_LAST = (((1,), (1,)), ((), ()))
FIRST_FIRST = (((0,), (0,)), ((), ()))
ROWS_COLS = (((1,), (0,)), ((), ()))


def partner(index, step, count):
    if count & (count - 1) == 0:
        return index ^ step
    return (index + step) % count


def origin(index, step, count):
    if count & (count - 1) == 0:
        return index ^ step
    return (index - step) % count


def pairs_of(owners):
    inner = 2 if owners % 2 == 0 else 1
    return inner, owners // inner


def source(me, block, owners):
    inner, outer = pairs_of(owners)
    return origin(me // inner, block // inner, outer) * inner + (me % inner ^ block % inner)


def exchange(value, axis, step):
    count = lax.axis_size(axis)
    return lax.ppermute(value, axis, [(i, partner(i, step, count)) for i in range(count)])


def to_sibling(value):
    return lax.ppermute(value, "expert", [(i, i ^ 1) for i in range(lax.axis_size("expert"))])


def to_pair(value, step, back=False):
    owners = lax.axis_size("expert")
    inner, outer = pairs_of(owners)
    hops = [(i, partner(i // inner, step, outer) * inner + i % inner) for i in range(owners)]
    return lax.ppermute(value, "expert", [(j, i) for i, j in hops] if back else hops)


def to_previous(value):
    count = lax.axis_size("pipe")
    return lax.ppermute(value, "pipe", [(i, (i - 1) % count) for i in range(count)])


def mm(left, right, dims):
    return lax.dot_general(left, right, dims, preferred_element_type=F32)


def run(body, name, outs, inputs, flops, moved=None, in_specs=None, out_specs=None, scratch=(), aliases=None):
    vmem = pl.BlockSpec(memory_space=pltpu.VMEM)
    if moved is None:
        moved = sum(v.size * v.dtype.itemsize for v in inputs)
    return pl.pallas_call(
        body,
        name=name,
        out_shape=outs,
        in_specs=in_specs or [vmem] * len(inputs),
        out_specs=out_specs or [vmem] * len(outs),
        scratch_shapes=scratch,
        input_output_aliases=aliases or {},
        compiler_params=pltpu.CompilerParams(vmem_limit_bytes=VMEM_LIMIT),
        cost_estimate=pl.CostEstimate(flops=flops, bytes_accessed=moved, transcendentals=0),
    )(*inputs)


def in_hbm(value):
    return pltpu.with_memory_space_constraint(value, pltpu.HBM)


def earlier_count(flags):
    lanes = flags.shape[1]
    before = lax.broadcasted_iota(jnp.int32, (lanes, lanes), 0) < lax.broadcasted_iota(jnp.int32, (lanes, lanes), 1)
    return mm(flags.astype(BF16), jnp.where(before, F32(1.0), F32(0.0)).astype(BF16), ROWS_COLS)


def one_hot(wanted, rows):
    number = lax.broadcasted_iota(jnp.int32, (rows, wanted.shape[1]), 0).astype(F32)
    return jnp.where(number == wanted[:1], F32(1.0), F32(0.0))


def sorting(early_row, late_row, tokens, capacity):
    early = one_hot(early_row, tokens - capacity)
    return jnp.concatenate([early, one_hot(late_row, capacity)], axis=0).astype(BF16)


def choose_late(routing, gates, capacity):
    tokens = routing.shape[1]
    matches = routing == 0
    member = jnp.max(jnp.where(matches, F32(1.0), F32(0.0)), axis=0, keepdims=True)
    share = jnp.sum(jnp.where(matches, gates, F32(0.0)), axis=0, keepdims=True)
    spread = jnp.broadcast_to(member, (capacity, tokens))
    slot = earlier_count(spread)
    members = jnp.sum(spread, axis=1, keepdims=True)
    rank = lax.broadcasted_iota(jnp.int32, (capacity, tokens), 1).astype(F32) - slot
    left = rank - F32(tokens - capacity)
    is_late = jnp.where((spread > 0.5) | (left >= 0.0), F32(1.0), F32(0.0))
    late_row = jnp.where(is_late > 0.5, jnp.where(spread > 0.5, slot, members + left), F32(-1.0))
    weighting = jnp.sum(one_hot(late_row, capacity) * share, axis=1, keepdims=True)
    return jnp.where(is_late > 0.5, F32(-1.0), rank), late_row, weighting


def store_late(both, weighting, incoming, picked_ref, routed_ref):
    picked = mm(both[-picked_ref.shape[0] :], incoming, ROWS_COLS)
    picked_ref[...] = picked.astype(BF16)
    routed_ref[...] = (picked * weighting).astype(BF16)


def route_body(
    routing_hbm,
    gates_hbm,
    incoming_hbm,
    early_ref,
    picked_ref,
    routed_ref,
    both_ref,
    weighting_ref,
    ids_ref,
    incoming_ref,
    routing_ref,
    gates_ref,
    sems,
):
    capacity, width = routed_ref.shape
    fetches = [
        pltpu.make_async_copy(routing_hbm, routing_ref, sems.at[0]),
        pltpu.make_async_copy(gates_hbm, gates_ref, sems.at[1]),
        pltpu.make_async_copy(incoming_hbm, incoming_ref, sems.at[2]),
    ]
    for f in reversed(fetches):
        f.start()
    for f in fetches[:2]:
        f.wait()
    early = early_ref.shape[0]
    early_row, late_row, weighting = choose_late(routing_ref[...], gates_ref[...], capacity)
    both = sorting(early_row, late_row, early + capacity, capacity)
    both_ref[...] = both
    weighting_ref[...] = jnp.broadcast_to(weighting, weighting_ref.shape)
    digits = [d for row in (early_row, late_row) for d in (row.astype(jnp.int32) >> 7, row.astype(jnp.int32) & 127)]
    number = lax.broadcasted_iota(jnp.int32, ids_ref.shape, 0)
    ids = digits[3]
    for i in range(3):
        ids = jnp.where(number == i, digits[i], ids)
    ids_ref[...] = ids.astype(F32).astype(BF16)
    fetches[2].wait()
    step = min(width, 1024)
    for c in range(width // step):
        at = slice(c * step, (c + 1) * step)
        early_ref[:, at] = mm(both[:early], incoming_ref[:, at], ROWS_COLS).astype(BF16)

    @pl.when(lax.axis_index("pipe") == 0)
    def _():
        store_late(both, weighting, incoming_ref[...], picked_ref, routed_ref)


def route_late_body(incoming_ref, both_ref, weighting_ref, _, __, picked_ref, routed_ref):
    @pl.when(lax.axis_index("pipe") > 0)
    def _():
        store_late(both_ref[...], weighting_ref[:, :1], incoming_ref[...], picked_ref, routed_ref)


def forward_body(saved_ref, weights_ref, slope_ref, active_ref, hidden_ref, rows_ref, *fars):
    owners, capacity, _ = saved_ref.shape
    others = len(fars)
    inner, outer = pairs_of(owners)
    me = lax.axis_index("expert")
    replica = lax.axis_index("dp")
    for k in range(owners):
        rows_ref[k * capacity : (k + 1) * capacity] = saved_ref[source(me, k, owners)]
    for r in range(others):
        part = fars[r].shape[1]
        first = pl.multiple_of(partner(replica, r + 1, others + 1) * part, LANES)
        for j in range(outer):
            fars[r][j * capacity : (j + 1) * capacity] = saved_ref[source(me, j * inner, owners), :, pl.ds(first, part)]
    rows = rows_ref[...]
    gate_pre = mm(weights_ref[0], rows, LAST_LAST)
    up_pre = mm(weights_ref[1], rows, LAST_LAST)
    sigmoid_gate = jax.nn.sigmoid(gate_pre)
    activated = gate_pre * sigmoid_gate
    slope_ref[...] = up_pre * sigmoid_gate * (1.0 + gate_pre * (1.0 - sigmoid_gate))
    active_ref[...] = activated
    hidden_ref[...] = jnp.transpose(activated * up_pre).astype(BF16)


def backward_body(order, *refs):
    blocks = refs[:order]
    weights_ref, slope_ref, active_ref, hidden_ref = refs[order : order + 4]
    kept_ref, grads_ref, *given = refs[order + 4 :]
    inner, outer = pairs_of(order)
    rows = jnp.concatenate([b[...] for b in blocks], axis=0)
    hidden_grad = mm(weights_ref[2], rows, LAST_LAST)
    gate_grad = jnp.transpose(hidden_grad * slope_ref[...]).astype(BF16)
    up_grad = jnp.transpose(hidden_grad * active_ref[...]).astype(BF16)
    capacity, width = blocks[0].shape
    step = 512
    for c in range(width // step):
        at = slice(c * step, (c + 1) * step)
        total = mm(gate_grad, weights_ref[0, :, at], ROWS_COLS) + mm(up_grad, weights_ref[1, :, at], ROWS_COLS)
        for k in range(order):
            j = k // inner
            block = total[k * capacity : (k + 1) * capacity].astype(BF16)
            if k % inner:
                given[j][:, at] = block
            else:
                kept_ref[j * capacity : (j + 1) * capacity, at] = block
    hid = weights_ref.shape[1]
    grads_ref[:, :hid] = gate_grad
    grads_ref[:, hid : 2 * hid] = up_grad
    grads_ref[:, 2 * hid :] = hidden_ref[...]


def pair_body(outer, paired, kept_ref, *refs):
    given, outs = refs[: outer - 1] if paired else (), refs[1 - outer :]
    capacity = outs[0].shape[0]
    for j, ref in enumerate(outs, 1):
        total = kept_ref[j * capacity : (j + 1) * capacity].astype(F32)
        if paired:
            total = total + given[j - 1][...].astype(F32)
        ref[...] = total.astype(BF16)


def pack_body(outer, *refs):
    blocks, fars = refs[:outer], refs[outer:]
    capacity = blocks[0].shape[0]
    part = fars[0].shape[1]
    replica = lax.axis_index("dp")
    for r, into in enumerate(fars, 1):
        first = pl.multiple_of(partner(replica, r, len(fars) + 1) * part, LANES)
        for j in range(outer):
            into[j * capacity : (j + 1) * capacity] = blocks[j][:, pl.ds(first, part)]


def return_body(picked_ref, ids_ref, kept_ref, *refs):
    returned, out_ref = refs[:-1], refs[-1]
    capacity, width = picked_ref.shape
    back = kept_ref[:capacity].astype(F32)
    for ref in returned:
        back = back + ref[...].astype(F32)
    out_ref[:, :width] = (picked_ref[...].astype(F32) + back).astype(BF16)
    out_ref[:, width:] = ids_ref[...]


def weight_body(others, owners, factors_ref, inputs_ref, *refs):
    inner, outer = pairs_of(owners)
    halves = others * inner
    blocks, refs = refs[:owners], refs[owners:]
    far_inputs, far_rows, far_factors = refs[:halves], refs[halves : 2 * halves], refs[2 * halves : 2 * halves + others]
    out_hbm, held, sems = refs[2 * halves + others :]
    capacity = blocks[0].shape[0]
    hid, part = out_hbm.shape[2:]
    columns = held.shape[2]
    replica = lax.axis_index("dp")
    left = [
        jnp.concatenate([f[:, i * hid : (i + 1) * hid] for f in (factors_ref, *far_factors)], axis=0) for i in range(3)
    ]

    def far(halves_of, at):
        return [
            halves_of[r * inner + i][j * capacity : (j + 1) * capacity, at]
            for r in range(others)
            for j in range(outer)
            for i in range(inner)
        ]

    copies = []
    for c in range(part // columns):
        at = slice(c * columns, (c + 1) * columns)
        own = pl.ds(pl.multiple_of(replica * part + c * columns, LANES), columns)
        inputs = jnp.concatenate([inputs_ref[:, own]] + far(far_inputs, at), axis=0)
        rows = jnp.concatenate([b[:, own] for b in blocks] + far(far_rows, at), axis=0)
        for i in range(3):
            n = len(copies)
            held[n] = mm(left[i], rows if i == 2 else inputs, FIRST_FIRST).astype(BF16)
            copies.append(pltpu.make_async_copy(held.at[n], out_hbm.at[0, i, :, pl.ds(c * columns, columns)], sems.at[n]))
            copies[-1].start()
    for c in copies:
        c.wait()


def merge_body(early_ref, changed_ref, out_hbm, held, sems):
    early, width = early_ref.shape
    capacity = changed_ref.shape[0]
    tokens = early + capacity
    digits = [changed_ref[:, width:][i : i + 1].astype(F32) for i in range(4)]
    both = sorting(digits[0] * 128.0 + digits[1], digits[2] * 128.0 + digits[3], tokens, capacity)
    step = held.shape[2]
    copies = []
    for c in range(width // step):
        at = slice(c * step, (c + 1) * step)
        rows = jnp.concatenate([early_ref[:, at], changed_ref[:, at]], axis=0)
        held[c] = mm(both, rows, FIRST_FIRST).astype(BF16)
        copies.append(pltpu.make_async_copy(held.at[c], out_hbm.at[0, 0, :, pl.ds(c * step, step)], sems.at[c]))
        copies[-1].start()
    for c in copies:
        c.wait()


def shards(output_grads, gate_values, routing, saved_inputs, expert_weights):
    owners = lax.axis_size("expert")
    replicas = lax.axis_size("dp")
    others = replicas - 1
    capacity = saved_inputs.shape[4]
    incoming = output_grads[0, 0]
    tokens, width = incoming.shape
    part = width // replicas
    weights = expert_weights[0]
    hid = weights.shape[1]
    rows = owners * capacity
    top = routing.shape[3]
    inner, outer = pairs_of(owners)
    mine = outer * capacity
    out = jax.ShapeDtypeStruct
    hbm = pl.BlockSpec(memory_space=pltpu.HBM)
    saved = saved_inputs[0, 0, 0]

    early = tokens - capacity
    late_outs = [out((capacity, width), BF16)] * 2
    early_rows, picked, routed, both, weighting, ids, incoming = run(
        route_body,
        "route",
        [
            out((early, width), BF16),
            *late_outs,
            out((tokens, tokens), BF16),
            out((capacity, LANES), F32),
            out((capacity, tokens), BF16),
            out((tokens, width), BF16),
        ],
        [in_hbm(v) for v in (jnp.transpose(routing[0, 0]), jnp.transpose(gate_values[0, 0]), incoming)],
        0,
        moved=0,
        in_specs=[hbm] * 3,
        scratch=[pltpu.VMEM((top, tokens), jnp.int32), pltpu.VMEM((top, tokens), F32), pltpu.SemaphoreType.DMA((3,))],
    )
    shifted = to_previous(early_rows)
    picked, routed = run(
        route_late_body,
        "route_late",
        late_outs,
        [incoming, both, weighting, picked, routed],
        ROUTE_COST,
        aliases={3: 0, 4: 1},
    )
    distant = [to_pair(routed, j) for j in range(1, outer)]
    arrived = [to_sibling(routed)] if inner == 2 else []

    def both_halves(values):
        return [h for v in values for h in ((v, to_sibling(v)) if inner == 2 else (v,))]

    slope, active, hidden, own_inputs, *fars = run(
        forward_body,
        "forward",
        [out((hid, rows), F32), out((hid, rows), F32), out((rows, hid), BF16), out((rows, width), BF16)]
        + [out((mine, part), BF16)] * others,
        [saved, weights],
        4 * rows * hid * width,
    )
    far_inputs = [exchange(f, "dp", k + 1) for k, f in enumerate(fars)]
    *distant, hidden = lax.optimization_barrier((*distant, hidden))
    for block in distant:
        arrived.append(block)
        if inner == 2:
            arrived.append(to_sibling(block))

    fars = run(
        functools.partial(pack_body, outer),
        "pack",
        [out((mine, part), BF16)] * others,
        [routed, *distant],
        0,
    )
    far_rows = both_halves([exchange(f, "dp", k + 1) for k, f in enumerate(fars)])
    far_inputs = both_halves(far_inputs)

    kept, grads, *given = run(
        functools.partial(backward_body, owners),
        "backward",
        [out((mine, width), BF16), out((rows, 3 * hid), BF16)] + [out((capacity, width), BF16)] * ((inner - 1) * outer),
        [routed, *arrived, weights, slope, active, hidden],
        6 * rows * hid * width,
    )
    given = [to_sibling(v) for v in given]
    sums = run(
        functools.partial(pair_body, outer, inner == 2),
        "pair_sums",
        [out((capacity, width), BF16)] * (outer - 1),
        [kept, *given[1:], *far_inputs[::inner]],
        0,
    )
    returned = [to_pair(v, j, back=True) for j, v in enumerate(sums, 1)]
    far_grads = [exchange(grads, "dp", k) for k in range(1, replicas)]

    changed = run(
        return_body,
        "sum_returned",
        [out((capacity, width + tokens), BF16)],
        [picked, ids, kept, *given[:1], *returned],
        0,
    )[0]
    next_changed = to_previous(changed)

    columns = min(part, 512)
    pieces = 3 * part // columns
    weight_grads = run(
        functools.partial(weight_body, others, owners),
        "weight_grads",
        [out((1, 3, hid, part), BF16)],
        [grads, own_inputs, routed, *arrived, *far_inputs, *far_rows, *far_grads],
        6 * rows * replicas * hid * part,
        out_specs=[hbm],
        scratch=[pltpu.VMEM((pieces, hid, columns), BF16), pltpu.SemaphoreType.DMA((pieces,))],
    )[0]

    step = min(width, 1024)
    passed_grads = run(
        merge_body,
        "merge",
        [out((1, 1, tokens, width), BF16)],
        [shifted, next_changed],
        2 * capacity * tokens * width,
        out_specs=[hbm],
        scratch=[pltpu.VMEM((width // step, tokens, step), BF16), pltpu.SemaphoreType.DMA((width // step,))],
    )[0]
    return (passed_grads, weight_grads)


def solution(mesh):
    placed = (
        P("dp", "pipe", "expert", None),
        P("dp", "pipe", "expert", None),
        P("dp", "pipe", "expert", None),
        P("dp", "pipe", None, None, None, None),
        P("pipe", None, "expert", None),
    )
    return jax.shard_map(
        shards,
        mesh=mesh,
        in_specs=placed,
        out_specs=(P("dp", "pipe", "expert", None), P("pipe", None, "expert", "dp")),
        check_vma=False,
    )
```

```python
import functools

import jax
import jax.numpy as jnp
from jax import lax
from jax.experimental import pallas as pl
from jax.experimental.pallas import tpu as pltpu
from jax.sharding import PartitionSpec as P

BF16 = jnp.bfloat16
F32 = jnp.float32
LANES = 128
VMEM_LIMIT = 12 * 2**20
ROUTE_COST = 10**10
LAST_LAST = (((1,), (1,)), ((), ()))
FIRST_FIRST = (((0,), (0,)), ((), ()))
ROWS_COLS = (((1,), (0,)), ((), ()))


def partner(index, step, count):
    if count & (count - 1) == 0:
        return index ^ step
    return (index + step) % count


def origin(index, step, count):
    if count & (count - 1) == 0:
        return index ^ step
    return (index - step) % count


def pairs_of(owners):
    inner = 2 if owners % 2 == 0 else 1
    return inner, owners // inner


def source(me, block, owners):
    inner, outer = pairs_of(owners)
    return origin(me // inner, block // inner, outer) * inner + (me % inner ^ block % inner)


def exchange(value, axis, step):
    count = lax.axis_size(axis)
    return lax.ppermute(value, axis, [(i, partner(i, step, count)) for i in range(count)])


def to_sibling(value):
    return lax.ppermute(value, "expert", [(i, i ^ 1) for i in range(lax.axis_size("expert"))])


def to_pair(value, step, back=False):
    owners = lax.axis_size("expert")
    inner, outer = pairs_of(owners)
    hops = [(i, partner(i // inner, step, outer) * inner + i % inner) for i in range(owners)]
    return lax.ppermute(value, "expert", [(j, i) for i, j in hops] if back else hops)


def to_previous(value):
    count = lax.axis_size("pipe")
    return lax.ppermute(value, "pipe", [(i, (i - 1) % count) for i in range(count)])


def mm(left, right, dims):
    return lax.dot_general(left, right, dims, preferred_element_type=F32)


def run(body, name, outs, inputs, flops, moved=None, in_specs=None, out_specs=None, scratch=(), aliases=None):
    vmem = pl.BlockSpec(memory_space=pltpu.VMEM)
    if moved is None:
        moved = sum(v.size * v.dtype.itemsize for v in inputs)
    return pl.pallas_call(
        body,
        name=name,
        out_shape=outs,
        in_specs=in_specs or [vmem] * len(inputs),
        out_specs=out_specs or [vmem] * len(outs),
        scratch_shapes=scratch,
        input_output_aliases=aliases or {},
        compiler_params=pltpu.CompilerParams(vmem_limit_bytes=VMEM_LIMIT),
        cost_estimate=pl.CostEstimate(flops=flops, bytes_accessed=moved, transcendentals=0),
    )(*inputs)


def in_hbm(value):
    return pltpu.with_memory_space_constraint(value, pltpu.HBM)


def earlier_count(flags):
    lanes = flags.shape[1]
    before = lax.broadcasted_iota(jnp.int32, (lanes, lanes), 0) < lax.broadcasted_iota(jnp.int32, (lanes, lanes), 1)
    return mm(flags.astype(BF16), jnp.where(before, F32(1.0), F32(0.0)).astype(BF16), ROWS_COLS)


def one_hot(wanted, rows):
    number = lax.broadcasted_iota(jnp.int32, (rows, wanted.shape[1]), 0).astype(F32)
    return jnp.where(number == wanted[:1], F32(1.0), F32(0.0))


def sorting(early_row, late_row, tokens, capacity):
    early = one_hot(early_row, tokens - capacity)
    return jnp.concatenate([early, one_hot(late_row, capacity)], axis=0).astype(BF16)


def choose_late(routing, gates, capacity):
    tokens = routing.shape[1]
    matches = routing == 0
    member = jnp.max(jnp.where(matches, F32(1.0), F32(0.0)), axis=0, keepdims=True)
    share = jnp.sum(jnp.where(matches, gates, F32(0.0)), axis=0, keepdims=True)
    spread = jnp.broadcast_to(member, (capacity, tokens))
    slot = earlier_count(spread)
    members = jnp.sum(spread, axis=1, keepdims=True)
    rank = lax.broadcasted_iota(jnp.int32, (capacity, tokens), 1).astype(F32) - slot
    left = rank - F32(tokens - capacity)
    is_late = jnp.where((spread > 0.5) | (left >= 0.0), F32(1.0), F32(0.0))
    late_row = jnp.where(is_late > 0.5, jnp.where(spread > 0.5, slot, members + left), F32(-1.0))
    weighting = jnp.sum(one_hot(late_row, capacity) * share, axis=1, keepdims=True)
    return jnp.where(is_late > 0.5, F32(-1.0), rank), late_row, weighting


def store_late(both, weighting, incoming, picked_ref, routed_ref):
    picked = mm(both[-picked_ref.shape[0] :], incoming, ROWS_COLS)
    picked_ref[...] = picked.astype(BF16)
    routed_ref[...] = (picked * weighting).astype(BF16)


def route_body(
    routing_hbm,
    gates_hbm,
    incoming_hbm,
    early_ref,
    picked_ref,
    routed_ref,
    both_ref,
    weighting_ref,
    ids_ref,
    incoming_ref,
    routing_ref,
    gates_ref,
    sems,
):
    capacity, width = routed_ref.shape
    fetches = [
        pltpu.make_async_copy(routing_hbm, routing_ref, sems.at[0]),
        pltpu.make_async_copy(gates_hbm, gates_ref, sems.at[1]),
        pltpu.make_async_copy(incoming_hbm, incoming_ref, sems.at[2]),
    ]
    for f in reversed(fetches):
        f.start()
    for f in fetches[:2]:
        f.wait()
    early = early_ref.shape[0]
    early_row, late_row, weighting = choose_late(routing_ref[...], gates_ref[...], capacity)
    both = sorting(early_row, late_row, early + capacity, capacity)
    both_ref[...] = both
    weighting_ref[...] = jnp.broadcast_to(weighting, weighting_ref.shape)
    digits = [d for row in (early_row, late_row) for d in (row.astype(jnp.int32) >> 7, row.astype(jnp.int32) & 127)]
    number = lax.broadcasted_iota(jnp.int32, ids_ref.shape, 0)
    ids = digits[3]
    for i in range(3):
        ids = jnp.where(number == i, digits[i], ids)
    ids_ref[...] = ids.astype(F32).astype(BF16)
    fetches[2].wait()
    step = min(width, 1024)
    for c in range(width // step):
        at = slice(c * step, (c + 1) * step)
        early_ref[:, at] = mm(both[:early], incoming_ref[:, at], ROWS_COLS).astype(BF16)

    @pl.when(lax.axis_index("pipe") == 0)
    def _():
        store_late(both, weighting, incoming_ref[...], picked_ref, routed_ref)


def route_late_body(incoming_ref, both_ref, weighting_ref, _, __, picked_ref, routed_ref):
    @pl.when(lax.axis_index("pipe") > 0)
    def _():
        store_late(both_ref[...], weighting_ref[:, :1], incoming_ref[...], picked_ref, routed_ref)


def forward_body(saved_ref, weights_ref, slope_ref, active_ref, hidden_ref, rows_ref, *fars):
    owners, capacity, _ = saved_ref.shape
    others = len(fars)
    inner, outer = pairs_of(owners)
    me = lax.axis_index("expert")
    replica = lax.axis_index("dp")
    for k in range(owners):
        rows_ref[k * capacity : (k + 1) * capacity] = saved_ref[source(me, k, owners)]
    for r in range(others):
        part = fars[r].shape[1]
        first = pl.multiple_of(partner(replica, r + 1, others + 1) * part, LANES)
        for j in range(outer):
            fars[r][j * capacity : (j + 1) * capacity] = saved_ref[source(me, j * inner, owners), :, pl.ds(first, part)]
    rows = rows_ref[...]
    gate_pre = mm(weights_ref[0], rows, LAST_LAST)
    up_pre = mm(weights_ref[1], rows, LAST_LAST)
    sigmoid_gate = jax.nn.sigmoid(gate_pre)
    activated = gate_pre * sigmoid_gate
    slope_ref[...] = up_pre * sigmoid_gate * (1.0 + gate_pre * (1.0 - sigmoid_gate))
    active_ref[...] = activated
    hidden_ref[...] = jnp.transpose(activated * up_pre).astype(BF16)


def backward_body(order, *refs):
    blocks = refs[:order]
    weights_ref, slope_ref, active_ref, hidden_ref = refs[order : order + 4]
    kept_ref, grads_ref, *given = refs[order + 4 :]
    inner, outer = pairs_of(order)
    rows = jnp.concatenate([b[...] for b in blocks], axis=0)
    hidden_grad = mm(weights_ref[2], rows, LAST_LAST)
    gate_grad = jnp.transpose(hidden_grad * slope_ref[...]).astype(BF16)
    up_grad = jnp.transpose(hidden_grad * active_ref[...]).astype(BF16)
    capacity, width = blocks[0].shape
    step = 512
    for c in range(width // step):
        at = slice(c * step, (c + 1) * step)
        total = mm(gate_grad, weights_ref[0, :, at], ROWS_COLS) + mm(up_grad, weights_ref[1, :, at], ROWS_COLS)
        for k in range(order):
            j = k // inner
            block = total[k * capacity : (k + 1) * capacity].astype(BF16)
            if k % inner:
                given[j][:, at] = block
            else:
                kept_ref[j * capacity : (j + 1) * capacity, at] = block
    hid = weights_ref.shape[1]
    grads_ref[:, :hid] = gate_grad
    grads_ref[:, hid : 2 * hid] = up_grad
    grads_ref[:, 2 * hid :] = hidden_ref[...]


def pair_body(outer, paired, kept_ref, *refs):
    given, outs = refs[: outer - 1] if paired else (), refs[1 - outer :]
    capacity = outs[0].shape[0]
    for j, ref in enumerate(outs, 1):
        total = kept_ref[j * capacity : (j + 1) * capacity].astype(F32)
        if paired:
            total = total + given[j - 1][...].astype(F32)
        ref[...] = total.astype(BF16)


def pack_body(outer, *refs):
    blocks, fars = refs[:outer], refs[outer:]
    capacity = blocks[0].shape[0]
    part = fars[0].shape[1]
    replica = lax.axis_index("dp")
    for r, into in enumerate(fars, 1):
        first = pl.multiple_of(partner(replica, r, len(fars) + 1) * part, LANES)
        for j in range(outer):
            into[j * capacity : (j + 1) * capacity] = blocks[j][:, pl.ds(first, part)]


def return_body(picked_ref, ids_ref, kept_ref, *refs):
    returned, out_ref = refs[:-1], refs[-1]
    capacity, width = picked_ref.shape
    back = kept_ref[:capacity].astype(F32)
    for ref in returned:
        back = back + ref[...].astype(F32)
    out_ref[:, :width] = (picked_ref[...].astype(F32) + back).astype(BF16)
    out_ref[:, width:] = ids_ref[...]


def weight_body(others, owners, factors_ref, inputs_ref, *refs):
    inner, outer = pairs_of(owners)
    halves = others * inner
    blocks, refs = refs[:owners], refs[owners:]
    far_inputs, far_rows, far_factors = refs[:halves], refs[halves : 2 * halves], refs[2 * halves : 2 * halves + others]
    out_hbm, held, sems = refs[2 * halves + others :]
    capacity = blocks[0].shape[0]
    hid, part = out_hbm.shape[2:]
    columns = held.shape[2]
    replica = lax.axis_index("dp")
    left = [
        jnp.concatenate([f[:, i * hid : (i + 1) * hid] for f in (factors_ref, *far_factors)], axis=0) for i in range(3)
    ]

    def far(halves_of, at):
        return [
            halves_of[r * inner + i][j * capacity : (j + 1) * capacity, at]
            for r in range(others)
            for j in range(outer)
            for i in range(inner)
        ]

    copies = []
    for c in range(part // columns):
        at = slice(c * columns, (c + 1) * columns)
        own = pl.ds(pl.multiple_of(replica * part + c * columns, LANES), columns)
        inputs = jnp.concatenate([inputs_ref[:, own]] + far(far_inputs, at), axis=0)
        rows = jnp.concatenate([b[:, own] for b in blocks] + far(far_rows, at), axis=0)
        for i in range(3):
            n = len(copies)
            held[n] = mm(left[i], rows if i == 2 else inputs, FIRST_FIRST).astype(BF16)
            copies.append(pltpu.make_async_copy(held.at[n], out_hbm.at[0, i, :, pl.ds(c * columns, columns)], sems.at[n]))
            copies[-1].start()
    for c in copies:
        c.wait()


def merge_pieces(width):
    return [width // 8] * 2 + [width // 4] * 3


def merge_body(early_ref, changed_ref, out_hbm, held, sems):
    early, width = early_ref.shape
    capacity = changed_ref.shape[0]
    tokens = early + capacity
    digits = [changed_ref[:, width:][i : i + 1].astype(F32) for i in range(4)]
    both = sorting(digits[0] * 128.0 + digits[1], digits[2] * 128.0 + digits[3], tokens, capacity)
    copies = []
    first = 0
    for n, piece in enumerate(merge_pieces(width)):
        at = pl.ds(first, piece)
        rows = jnp.concatenate([early_ref[:, at], changed_ref[:, at]], axis=0)
        held[:, at] = mm(both, rows, FIRST_FIRST).astype(BF16)
        copies.append(pltpu.make_async_copy(held.at[:, at], out_hbm.at[0, 0, :, at], sems.at[n]))
        copies[-1].start()
        first += piece
    for c in copies:
        c.wait()


def shards(output_grads, gate_values, routing, saved_inputs, expert_weights):
    owners = lax.axis_size("expert")
    replicas = lax.axis_size("dp")
    others = replicas - 1
    capacity = saved_inputs.shape[4]
    incoming = output_grads[0, 0]
    tokens, width = incoming.shape
    part = width // replicas
    weights = expert_weights[0]
    hid = weights.shape[1]
    rows = owners * capacity
    top = routing.shape[3]
    inner, outer = pairs_of(owners)
    mine = outer * capacity
    out = jax.ShapeDtypeStruct
    hbm = pl.BlockSpec(memory_space=pltpu.HBM)
    saved = saved_inputs[0, 0, 0]

    early = tokens - capacity
    late_outs = [out((capacity, width), BF16)] * 2
    early_rows, picked, routed, both, weighting, ids, incoming = run(
        route_body,
        "route",
        [
            out((early, width), BF16),
            *late_outs,
            out((tokens, tokens), BF16),
            out((capacity, LANES), F32),
            out((capacity, tokens), BF16),
            out((tokens, width), BF16),
        ],
        [in_hbm(v) for v in (jnp.transpose(routing[0, 0]), jnp.transpose(gate_values[0, 0]), incoming)],
        0,
        moved=0,
        in_specs=[hbm] * 3,
        scratch=[pltpu.VMEM((top, tokens), jnp.int32), pltpu.VMEM((top, tokens), F32), pltpu.SemaphoreType.DMA((3,))],
    )
    shifted = to_previous(early_rows)
    picked, routed = run(
        route_late_body,
        "route_late",
        late_outs,
        [incoming, both, weighting, picked, routed],
        ROUTE_COST,
        aliases={3: 0, 4: 1},
    )
    distant = [to_pair(routed, j) for j in range(1, outer)]
    arrived = [to_sibling(routed)] if inner == 2 else []

    def both_halves(values):
        return [h for v in values for h in ((v, to_sibling(v)) if inner == 2 else (v,))]

    slope, active, hidden, own_inputs, *fars = run(
        forward_body,
        "forward",
        [out((hid, rows), F32), out((hid, rows), F32), out((rows, hid), BF16), out((rows, width), BF16)]
        + [out((mine, part), BF16)] * others,
        [saved, weights],
        4 * rows * hid * width,
    )
    far_inputs = [exchange(f, "dp", k + 1) for k, f in enumerate(fars)]
    *distant, hidden = lax.optimization_barrier((*distant, hidden))
    for block in distant:
        arrived.append(block)
        if inner == 2:
            arrived.append(to_sibling(block))

    fars = run(
        functools.partial(pack_body, outer),
        "pack",
        [out((mine, part), BF16)] * others,
        [routed, *distant],
        0,
    )
    far_rows = both_halves([exchange(f, "dp", k + 1) for k, f in enumerate(fars)])
    far_inputs = both_halves(far_inputs)

    kept, grads, *given = run(
        functools.partial(backward_body, owners),
        "backward",
        [out((mine, width), BF16), out((rows, 3 * hid), BF16)] + [out((capacity, width), BF16)] * ((inner - 1) * outer),
        [routed, *arrived, weights, slope, active, hidden],
        6 * rows * hid * width,
    )
    given = [to_sibling(v) for v in given]
    sums = run(
        functools.partial(pair_body, outer, inner == 2),
        "pair_sums",
        [out((capacity, width), BF16)] * (outer - 1),
        [kept, *given[1:], *far_inputs[::inner]],
        0,
    )
    returned = [to_pair(v, j, back=True) for j, v in enumerate(sums, 1)]
    far_grads = [exchange(grads, "dp", k) for k in range(1, replicas)]

    changed = run(
        return_body,
        "sum_returned",
        [out((capacity, width + tokens), BF16)],
        [picked, ids, kept, *given[:1], *returned],
        0,
    )[0]
    next_changed = to_previous(changed)

    columns = min(part, 512)
    pieces = 3 * part // columns
    weight_grads = run(
        functools.partial(weight_body, others, owners),
        "weight_grads",
        [out((1, 3, hid, part), BF16)],
        [grads, own_inputs, routed, *arrived, *far_inputs, *far_rows, *far_grads],
        6 * rows * replicas * hid * part,
        out_specs=[hbm],
        scratch=[pltpu.VMEM((pieces, hid, columns), BF16), pltpu.SemaphoreType.DMA((pieces,))],
    )[0]

    passed_grads = run(
        merge_body,
        "merge",
        [out((1, 1, tokens, width), BF16)],
        [shifted, next_changed],
        2 * capacity * tokens * width,
        out_specs=[hbm],
        scratch=[pltpu.VMEM((tokens, width), BF16), pltpu.SemaphoreType.DMA((len(merge_pieces(width)),))],
    )[0]
    return (passed_grads, weight_grads)


def solution(mesh):
    placed = (
        P("dp", "pipe", "expert", None),
        P("dp", "pipe", "expert", None),
        P("dp", "pipe", "expert", None),
        P("dp", "pipe", None, None, None, None),
        P("pipe", None, "expert", None),
    )
    return jax.shard_map(
        shards,
        mesh=mesh,
        in_specs=placed,
        out_specs=(P("dp", "pipe", "expert", None), P("pipe", None, "expert", "dp")),
        check_vma=False,
    )
```
